32 devices in a mesh: pipe: 8 (over y, x, core), xs: 4 (over z).
Axes of the slice: x: 2, y: 2, z: 4, core: 2. Of those that a mesh axis runs over, the one named last changes fastest.
Arguments:
- start_vectors: bfloat16 [64, 16, 32, 512], P('pipe', None, 'xs'), may hold values from -36 to 36
- diag_blocks: bfloat16 [32, 512, 512], P('xs'), may hold values from -0.125 to 0.125
- face_blocks: bfloat16 [32, 4, 64, 512], P('xs'), may hold values from -0.1875 to 0.1875
- axial_blocks: bfloat16 [8, 512, 512], replicated, may hold values from -0.0625 to 0.0625
- neighbor_ids: int32 [32, 4], P('xs'), may hold values from 0 to 31
- neighbor_face: int32 [32, 4], P('xs'), may hold values from 0 to 3
- face_mask: int32 [32, 4], P('xs'), may hold values 0 or 1
Outputs:
- filtered: bfloat16 [64, 16, 32, 512], P('pipe', None, 'xs')
- gram: float32 [16, 16], replicated
- projected: float32 [16, 16], replicated
The draws below stay inside these ranges and needn't reach their ends.
Inputs may be any that keep to these rules, and one draw needn't show every extreme that they name: `neighbor_ids`: an element number of the cross-section. `neighbor_face`: a face number.
All inputs are finite; a program needn't handle non-finite values. No bound on the sum of `face_mask` on one device may be relied on, other than what follows from the above.
Results may differ from the reference program's by a relative error of at most 0.0042.
Values may be sent and summed in bfloat16 or wider, within the bound.
No kernel may reach another device: no remote copies, remote signals or barrier semaphores. Data moves between devices by JAX's collectives and lax.ppermute only.
A program may use at most 192 MiB of HBM per device.

```python
import jax
import jax.numpy as jnp
from jax import lax

P_SIZE = 8
F = 4
HW = 4
NV = 16
B = 512
TR = 64
NL = 64
E = 32


def draw_start_vectors(key, part):
    key_noise, key_shared, key_scale = jax.random.split(jax.random.fold_in(key, 11), 3)
    column_scale = 0.3 * jnp.exp(jnp.log(10.0) * jax.random.uniform(key_scale, (1, NV, 1, 1), jnp.float32))
    layer_pos = jnp.arange(NL).astype(jnp.float32)[:, None, None, None] / NL
    rising = jnp.exp(0.5 * jnp.log(3.0) * layer_pos)
    noise = jnp.clip(jax.random.normal(key_noise, (NL, NV, E, B), jnp.float32), -4.0, 4.0)
    shared = jnp.clip(jax.random.normal(key_shared, (NL, 1, E, B), jnp.float32), -4.0, 4.0)
    base = noise + 0.7 * shared
    return (column_scale * rising * base).astype(jnp.bfloat16)


def plant(result, key, smallest, high):
    place = [jax.random.randint(jax.random.fold_in(key, axis), (), 0, length) for axis, length in enumerate(result.shape)]
    widest = result.shape.index(max(result.shape))
    neighbour = place[:widest] + [(place[widest] + 1) % result.shape[widest]] + place[widest + 1:]
    return result.at[tuple(place)].set(smallest).at[tuple(neighbour)].set(high)


def shard_levels(key, extent, shards, least, largest):
    loudness, own = 1.0, jax.random.fold_in(key, 6)
    for axis_at, blocks in shards:
        draws = jnp.exp(jax.random.uniform(jax.random.fold_in(own, axis_at), (blocks,), jnp.float32, least / len(shards), largest / len(shards)))
        loudness = loudness * jnp.repeat(draws, extent[axis_at] // blocks).reshape([-1 if axis == axis_at else 1 for axis in range(len(extent))])
    return loudness


def gaussian(key, dims, deviation, most, cuts=(), dtype=jnp.bfloat16):
    level = shard_levels(key, dims, cuts, -0.22, 0.18) if cuts else 1.0
    result = jax.random.normal(key, dims, jnp.float32) * deviation * level
    return jnp.minimum(jnp.maximum(result, -most), most).astype(dtype)


def setup_inputs(seed: int = 0) -> dict:
    arg_keys = jax.random.split(jax.random.key(seed), 8)
    return {
        "start_vectors": draw_start_vectors(jax.random.fold_in(arg_keys[7], 71), 0),
        "diag_blocks": gaussian(arg_keys[1], (E, B, B), (4 * B) ** -0.5, 0.125, ((0, 4),)),
        "face_blocks": gaussian(arg_keys[2], (E, F, TR, B), (4 * F * TR) ** -0.5, 0.1875, ((0, 4),)),
        "axial_blocks": gaussian(arg_keys[3], (2 * HW, B, B), (4 * HW * B) ** -0.5, 0.0625),
        "neighbor_ids": plant(jax.random.randint(arg_keys[4], (E, F), 0, E), jax.random.fold_in(arg_keys[4], 1), 0, E - 1).astype(jnp.int32),
        "neighbor_face": plant(jax.random.randint(arg_keys[5], (E, F), 0, F), jax.random.fold_in(arg_keys[5], 1), 0, F - 1).astype(jnp.int32),
        "face_mask": plant((jax.random.randint(arg_keys[6], (E, F), 0, 4) < 3).astype(jnp.int32), jax.random.fold_in(arg_keys[6], 1), 0, 1),
    }


def face_traces(vectors):
    layer_count, vector_count, element_count, block_width = vectors.shape
    cube = vectors.reshape(layer_count, vector_count, element_count, P_SIZE, P_SIZE, P_SIZE)
    stacked = jnp.stack([cube[:, :, :, 0], cube[:, :, :, P_SIZE - 1], cube[:, :, :, :, 0], cube[:, :, :, :, P_SIZE - 1]], axis=3)
    return stacked.reshape(layer_count, vector_count, element_count, F, P_SIZE * P_SIZE)


def operate(vectors, diag_blocks, face_blocks, axial_blocks, neighbor_ids, neighbor_face, face_mask):
    traces = face_traces(vectors)
    picked = traces[:, :, neighbor_ids, neighbor_face]
    picked = picked * face_mask.astype(jnp.bfloat16)[None, None, :, :, None]
    summed = jnp.einsum("lneb,ebc->lnec", vectors.astype(jnp.float32), diag_blocks.astype(jnp.float32), precision=lax.Precision.HIGHEST)
    summed = summed + jnp.einsum("lneft,eftc->lnec", picked.astype(jnp.float32), face_blocks.astype(jnp.float32), precision=lax.Precision.HIGHEST)
    block_width = vectors.shape[-1]
    for position in range(2 * HW):
        offset = position - HW if position < HW else position - HW + 1
        shifted = jnp.roll(vectors, -offset, axis=0)
        product = jnp.dot(shifted.reshape(-1, block_width), axial_blocks[position], preferred_element_type=jnp.float32)
        summed = summed + product.reshape(summed.shape)
    return summed


def reference(start_vectors, diag_blocks, face_blocks, axial_blocks, neighbor_ids, neighbor_face, face_mask):
    blocks = (diag_blocks, face_blocks, axial_blocks, neighbor_ids, neighbor_face, face_mask)
    first_image = operate(start_vectors, *blocks)
    first = ((first_image - 0.3 * start_vectors.astype(jnp.float32)) / 1.2).astype(jnp.bfloat16)
    second_image = operate(first, *blocks)
    filtered = (2.0 * (second_image - 0.3 * first.astype(jnp.float32)) / 1.2 - start_vectors.astype(jnp.float32)).astype(jnp.bfloat16)
    image = operate(filtered, *blocks)
    count_all = jnp.float32(NL * E * B)
    wide = filtered.astype(jnp.float32)
    gram = jnp.einsum("lneb,lmeb->nm", wide, wide, precision=lax.Precision.HIGHEST) / count_all
    projected = jnp.einsum("lneb,lmeb->nm", wide, image, precision=lax.Precision.HIGHEST) / count_all
    return filtered, gram, projected
```

```python
import functools

import jax
import jax.numpy as jnp
from jax import lax
from jax.experimental import pallas as pl
from jax.experimental.pallas import tpu as pltpu
from jax.sharding import PartitionSpec as P

P_SIZE = 8
F = 4
HW = 4
TR = P_SIZE * P_SIZE
LANES = 128
CHUNKS = 1
PAIR_CAP = 12
ROW_TILE = 256
VMEM_BYTES = 48 * 1024 * 1024

shift_center = 0.3
half_width = 1.2

VMEM = pl.BlockSpec(memory_space=pltpu.VMEM)
SMEM = pl.BlockSpec(memory_space=pltpu.SMEM)
ANY = pl.BlockSpec(memory_space=pl.ANY)
bf16 = jnp.bfloat16
f32 = jnp.float32


def dot(a, b):
    return jnp.dot(a, b, preferred_element_type=f32)


def trace_selector(block):
    node = lax.broadcasted_iota(jnp.int32, (block, F * TR), 0)
    column = lax.broadcasted_iota(jnp.int32, (block, F * TR), 1)
    face, entry = column // TR, column % TR
    major, minor = entry // P_SIZE, entry % P_SIZE
    fixed = jnp.where(face % 2 == 0, 0, P_SIZE - 1)
    on_i = fixed * TR + major * P_SIZE + minor
    on_j = major * TR + fixed * P_SIZE + minor
    return (node == jnp.where(face < 2, on_i, on_j)).astype(bf16)


def left_half(shape):
    return lax.broadcasted_iota(jnp.int32, shape, len(shape) - 1) < TR


def read_wide(ref, index):
    return jnp.concatenate([ref[k, index, :] for k in range(ref.shape[0])], axis=1)


def write_wide(ref, index, value):
    for k in range(ref.shape[0]):
        ref[k, index, :] = value[:, k * LANES : (k + 1) * LANES]


def of_element(ref, e, elements):
    return pl.ds(e, ref.shape[1] // elements, stride=elements)


def store_traces(wide_ref, selector, traces_ref, elements):
    half = wide_ref.shape[1] // elements // 2
    for e in range(elements):
        values = dot(read_wide(wide_ref, of_element(wide_ref, e, elements)).astype(bf16), selector)
        for pair in range(F // 2):
            a = values[:half, pair * LANES : (pair + 1) * LANES]
            b = values[half:, pair * LANES : (pair + 1) * LANES]
            left = left_half(a.shape)
            traces_ref[e * F + 2 * pair] = jnp.where(left, a, pltpu.roll(b, TR, 1)).astype(bf16)
            traces_ref[e * F + 2 * pair + 1] = jnp.where(left, pltpu.roll(a, TR, 1), b).astype(bf16)


def pick_traces(lists_ref, traces_ref, sent_refs):
    for shift, sent in enumerate(sent_refs):

        def body(j, carry, shift=shift, sent=sent):
            sent[j] = traces_ref[lists_ref[shift, j]]
            return carry

        lax.fori_loop(0, sent.shape[0], body, 0)


def lifted_rows(e, refs_ref, traces_ref, arrived_refs):
    per = traces_ref.shape[0]
    slots = []
    for f in range(F):
        code = refs_ref[0, e * F + f]
        source, place = code // per, code % per
        value = jnp.where(source == 0, traces_ref[place].astype(f32), 0.0)
        for shift, arrived in enumerate(arrived_refs):
            here = source == shift + 1
            value = jnp.where(here, arrived[jnp.where(here, place, 0)].astype(f32), value)
        slots.append(value)
    tops, bottoms = [], []
    for pair in range(F // 2):
        a, b = slots[2 * pair], slots[2 * pair + 1]
        left = left_half(a.shape)
        tops.append(jnp.where(left, a, pltpu.roll(b, TR, 1)))
        bottoms.append(jnp.where(left, pltpu.roll(a, TR, 1), b))
    both = jnp.concatenate([jnp.concatenate(tops, 1), jnp.concatenate(bottoms, 1)], 0)
    return both.astype(bf16)


def opening_kernel(start_ref, selector_ref, low_ref, high_ref, traces_ref, wide):
    layers, width, elements, block = start_ref.shape
    edge = low_ref.shape[0]
    values = start_ref[...].reshape(layers * width * elements, block)
    low_ref[...] = values[:edge]
    high_ref[...] = values[-edge:]
    write_wide(wide, slice(None), values.astype(f32))
    store_traces(wide, selector_ref[...], traces_ref, elements)


def picking_kernel(lists_ref, traces_ref, *sent_refs):
    pick_traces(lists_ref, traces_ref, sent_refs)


def pattern_kernel(*refs):
    codes_refs, (me_ref, lists_ref, places_ref, most_ref) = refs[:-4], refs[-4:]
    shards = len(codes_refs)
    per = codes_refs[0].shape[0]
    every = shards * per
    me = me_ref[0]
    lane = lax.broadcasted_iota(jnp.int32, (per, every), 1)
    asked = [codes[:, :1] == lane for codes in codes_refs]
    need = jnp.concatenate(
        [jnp.max(a.astype(f32), axis=0, keepdims=True) for a in asked]
        + [jnp.zeros((8 - shards % 8, every), f32)] * (shards % 8 != 0),
        axis=0,
    ).astype(bf16)
    row = lax.broadcasted_iota(jnp.int32, (every, every), 0)
    column = lax.broadcasted_iota(jnp.int32, (every, every), 1)
    same = row // per == column // per
    before = (same & (row < column)).astype(bf16)
    rank = dot(need, before)
    total = dot(need, same.astype(bf16))
    over = (((0,), (1,)), ((), ()))
    rank_down = lax.dot_general(before, need, over, preferred_element_type=f32)
    need_down = lax.dot_general((row == column).astype(bf16), need, over, preferred_element_type=f32)
    block_of = lax.broadcasted_iota(jnp.int32, total.shape, 1) // per
    asker = lax.rem(lax.broadcasted_iota(jnp.int32, total.shape, 0) + me, shards)
    most = jnp.max(jnp.max(jnp.where(block_of == asker, 0.0, total), axis=1, keepdims=True), axis=0, keepdims=True)
    most_ref[...] = jnp.broadcast_to(most, most_ref.shape).astype(jnp.int32)
    trace = lax.broadcasted_iota(jnp.int32, (every, LANES), 0)
    slot = lax.broadcasted_iota(jnp.int32, (every, LANES), 1)
    mine = trace // per == me
    lists_ref[...] = jnp.zeros_like(lists_ref)
    for shift in range(1, shards):
        sent = mine & (need_down[:, shift : shift + 1] > 0.5) & (
            rank_down[:, shift : shift + 1].astype(jnp.int32) == slot
        )
        listed = jnp.sum(jnp.where(sent, (trace - me * per).astype(f32), 0.0), axis=0, keepdims=True)
        lists_ref[shift - 1 : shift, :] = listed.astype(jnp.int32)
    owner = lax.rem(me + shards - lane // per, shards)
    place = jnp.where(owner == 0, lane % per, rank[:1].astype(jnp.int32))
    code = jnp.where(asked[0], owner * per + place, 0).astype(f32)
    found = jnp.sum(code, axis=1, keepdims=True)
    hit = jnp.sum(asked[0].astype(f32), axis=1, keepdims=True)
    found = jnp.where(hit > 0.5, found, float(every))
    down = lax.broadcasted_iota(jnp.int32, (per, LANES), 0)
    across = lax.broadcasted_iota(jnp.int32, (per, LANES), 1)
    turned = jnp.sum(jnp.where(down == across, jnp.broadcast_to(found, (per, LANES)), 0.0), axis=0, keepdims=True)
    places_ref[...] = turned.astype(jnp.int32)


def round_kernel(step, shards, elements, *refs):
    refs = list(refs)
    take = lambda n: [refs.pop(0) for _ in range(n)]
    places_ref, lists_ref, here_ref, low_ref, high_ref, traces_ref = take(6)
    arrived_refs = take(shards - 1)
    diag_hbm, face_hbm, axial_hbm, selector_ref = take(4)
    if step == 2:
        (start_ref,) = take(1)
    if step == 3:
        gram_ref, projected_ref = take(2)
    else:
        out_ref, out_low_ref, out_high_ref, out_traces_ref = take(4)
        sent_refs = take(shards - 1)
    ext, wide, acc, diag, face, axial, sems = refs
    rows, block = here_ref.shape
    edge = low_ref.shape[0]
    layer = edge // HW

    loads = [
        pltpu.make_async_copy(diag_hbm, diag, sems.at[0]),
        pltpu.make_async_copy(face_hbm, face, sems.at[1]),
        pltpu.make_async_copy(axial_hbm, axial, sems.at[2]),
    ]
    for load in loads:
        load.start()
    ext[:edge] = low_ref[...]
    ext[edge : edge + rows] = here_ref[...]
    ext[edge + rows :] = high_ref[...]
    write_wide(wide, slice(None), here_ref[...].astype(f32))
    loads[0].wait()
    loads[1].wait()
    for e in range(elements):
        own = read_wide(wide, of_element(wide, e, elements)).astype(bf16)
        lifted = lifted_rows(e, places_ref, traces_ref, arrived_refs)
        write_wide(acc, of_element(acc, e, elements), dot(own, diag[e]) + dot(lifted, face[e]))
    loads[2].wait()
    tile = min(ROW_TILE, rows)

    def along(i, carry):
        base = pl.multiple_of(i * tile, tile)
        sides = []
        for position in range(2 * HW):
            offset = position if position < HW else position + 1
            sides.append(ext[pl.ds(pl.multiple_of(base + offset * layer, 16), tile), :])
        total = read_wide(acc, pl.ds(base, tile)) + dot(jnp.concatenate(sides, 1), axial[...])
        here = here_ref[pl.ds(base, tile), :].astype(f32)
        if step == 1:
            new = (total - shift_center * here) * (1.0 / half_width)
        elif step == 2:
            begun = start_ref[pl.ds(base, tile), :].astype(f32)
            new = (total - shift_center * here) * (2.0 / half_width) - begun
        else:
            write_wide(acc, pl.ds(base, tile), total)
            return carry
        new = new.astype(bf16)
        out_ref[pl.ds(base, tile), :] = new
        write_wide(acc, pl.ds(base, tile), new.astype(f32))
        return carry

    lax.fori_loop(0, rows // tile, along, 0)
    if step != 3:
        out_low_ref[...] = out_ref[:edge]
        out_high_ref[...] = out_ref[rows - edge :]
        store_traces(acc, selector_ref[...], out_traces_ref, elements)
        pick_traces(lists_ref, out_traces_ref, sent_refs)
        return

    over = (((1,), (1,)), ((), ()))
    gram = jnp.zeros((layer, layer), f32)
    projected = jnp.zeros((layer, layer), f32)
    for l in range(rows // layer):
        own = here_ref[l * layer : (l + 1) * layer]
        image = read_wide(acc, slice(l * layer, (l + 1) * layer))
        upper = image.astype(bf16)
        lower = (image - upper.astype(f32)).astype(bf16)
        gram += lax.dot_general(own, own, over, preferred_element_type=f32)
        projected += lax.dot_general(own, upper, over, preferred_element_type=f32)
        projected += lax.dot_general(own, lower, over, preferred_element_type=f32)
    vectors = layer // elements
    down = lax.broadcasted_iota(jnp.int32, (layer, layer), 0)
    across = lax.broadcasted_iota(jnp.int32, (layer, layer), 1)
    keep = down % elements == across % elements
    group = (
        lax.broadcasted_iota(jnp.int32, (layer, LANES), 0) // elements
        == lax.broadcasted_iota(jnp.int32, (layer, LANES), 1)
    ).astype(f32)
    for ref, value in ((gram_ref, gram), (projected_ref, projected)):
        value = jnp.where(keep, value, 0.0).reshape(vectors, elements, layer).sum(1)
        ref[...] = jnp.dot(value, group, precision=lax.Precision.HIGHEST, preferred_element_type=f32)


def shape(dims, dtype=bf16):
    return jax.ShapeDtypeStruct(dims, dtype)


def params():
    return pltpu.CompilerParams(vmem_limit_bytes=VMEM_BYTES)


def rotate(value, axis, shift):
    count = lax.axis_size(axis)
    return lax.ppermute(value, axis, [(i, (i + shift) % count) for i in range(count)])


def add_over(value, axis):
    count = lax.axis_size(axis)
    if count & (count - 1):
        return lax.psum(value, axis)
    step = 1
    while step < count:
        value = value + lax.ppermute(value, axis, [(i, i ^ step) for i in range(count)])
        step *= 2
    return value


def local(start_vectors, diag_blocks, face_blocks, axial_blocks, neighbor_ids, neighbor_face, face_mask):
    layers, vectors, elements, block = start_vectors.shape
    shards = lax.axis_size("xs")
    me = lax.axis_index("xs").astype(jnp.int32)
    per = elements * F
    width = vectors
    rows = layers * width * elements
    edge = HW * width * elements
    half = layers * width // 2
    face_flat = face_blocks.reshape(elements, F * TR, block)
    axial_flat = axial_blocks.reshape(2 * HW * block, block)
    selector = trace_selector(block)

    codes = jnp.where(face_mask == 1, neighbor_ids * F + neighbor_face, -1).reshape(per, 1)
    codes = jnp.broadcast_to(codes, (per, LANES)).astype(jnp.int32)
    all_codes = [codes] + [rotate(codes, "xs", -shift) for shift in range(1, shards)]
    lists, places, most = pl.pallas_call(
        pattern_kernel,
        out_shape=[shape((8, LANES), jnp.int32), shape((1, LANES), jnp.int32), shape((1, LANES), jnp.int32)],
        in_specs=[VMEM] * shards + [SMEM],
        out_specs=[VMEM] * 3,
        compiler_params=params(),
        name="pattern",
    )(*all_codes, me.reshape(1))

    low, high, traces = pl.pallas_call(
        opening_kernel,
        out_shape=[shape((edge, block)), shape((edge, block)), shape((per, half, LANES))],
        in_specs=[VMEM] * 2,
        out_specs=[VMEM] * 3,
        scratch_shapes=[pltpu.VMEM((block // LANES, rows, LANES), f32)],
        compiler_params=params(),
        name="opening",
    )(start_vectors, selector)

    start_flat = start_vectors.reshape(rows, block)
    macs = rows * block * (block * (1 + 2 * HW) + F * TR)

    def one_round(step, cap, here, low, high, traces, sent):
        from_low = rotate(high, "pipe", 1)
        from_high = rotate(low, "pipe", -1)
        arrived = [rotate(s, "xs", shift + 1) for shift, s in enumerate(sent)]
        operands = [places, lists, here, from_low, from_high, traces, *arrived]
        operands += [diag_blocks, face_flat, axial_flat, selector]
        specs = [SMEM] * 2 + [VMEM] * (4 + shards - 1) + [ANY] * 3 + [VMEM]
        if step == 2:
            operands.append(start_flat)
            specs.append(VMEM)
        if step == 3:
            outs = [shape((vectors, LANES), f32)] * 2
        else:
            outs = [shape((rows, block)), shape((edge, block)), shape((edge, block)), shape((per, half, LANES))]
            outs += [shape((cap, half, LANES))] * (shards - 1)
        return pl.pallas_call(
            functools.partial(round_kernel, step, shards, elements),
            out_shape=outs,
            in_specs=specs,
            out_specs=[VMEM] * len(outs),
            scratch_shapes=[
                pltpu.VMEM((rows + 2 * edge, block), bf16),
                pltpu.VMEM((block // LANES, rows, LANES), f32),
                pltpu.VMEM((block // LANES, rows, LANES), f32),
                pltpu.VMEM((elements, block, block), bf16),
                pltpu.VMEM((elements, F * TR, block), bf16),
                pltpu.VMEM((2 * HW * block, block), bf16),
                pltpu.SemaphoreType.DMA((3,)),
            ],
            compiler_params=params(),
            cost_estimate=pl.CostEstimate(flops=2 * macs, bytes_accessed=14 * 2**20, transcendentals=0),
            name=f"round_{step}",
        )(*operands)

    def run(cap):
        sent = pl.pallas_call(
            picking_kernel,
            out_shape=[shape((cap, half, LANES))] * (shards - 1),
            in_specs=[SMEM, VMEM],
            out_specs=[VMEM] * (shards - 1),
            compiler_params=params(),
            name="picking",
        )(lists, traces)
        first, *rest = one_round(1, cap, start_flat, low, high, traces, sent)
        filtered, *rest = one_round(2, cap, first, rest[0], rest[1], rest[2], rest[3:])
        gram, projected = one_round(3, cap, filtered, rest[0], rest[1], rest[2], rest[3:])
        return filtered, gram, projected

    filtered, gram, projected = lax.cond(
        most[0, 0] <= PAIR_CAP, lambda: run(min(PAIR_CAP, per)), lambda: run(per)
    )
    both = jnp.concatenate([gram, projected], axis=0)
    both = add_over(add_over(both, "pipe"), "xs")
    count_all = float(layers * lax.axis_size("pipe") * elements * shards * block)
    both = both[:, :vectors] / count_all
    return filtered.reshape(start_vectors.shape), both[:vectors], both[vectors:]


def solution(mesh):
    in_specs = (
        P("pipe", None, "xs", None),
        P("xs", None, None),
        P("xs", None, None, None),
        P(),
        P("xs", None),
        P("xs", None),
        P("xs", None),
    )
    out_specs = (P("pipe", None, "xs", None), P(), P())
    return jax.shard_map(local, mesh=mesh, in_specs=in_specs, out_specs=out_specs, check_vma=False)
```

```python
import functools

import jax
import jax.numpy as jnp
from jax import lax
from jax.experimental import pallas as pl
from jax.experimental.pallas import tpu as pltpu
from jax.sharding import PartitionSpec as P

P_SIZE = 8
F = 4
HW = 4
TR = P_SIZE * P_SIZE
LANES = 128
CAPS = (9, 12)
ROW_TILE = 256
UNROLL = 8
NEAR = 2

shift_center = 0.3
half_width = 1.2

VMEM = pl.BlockSpec(memory_space=pltpu.VMEM)
SMEM = pl.BlockSpec(memory_space=pltpu.SMEM)
ANY = pl.BlockSpec(memory_space=pl.ANY)
bf16 = jnp.bfloat16
f32 = jnp.float32


def dot(a, b):
    return jnp.dot(a, b, preferred_element_type=f32)


def trace_selector(block):
    node = lax.broadcasted_iota(jnp.int32, (block, F * TR), 0)
    column = lax.broadcasted_iota(jnp.int32, (block, F * TR), 1)
    face, entry = column // TR, column % TR
    major, minor = entry // P_SIZE, entry % P_SIZE
    fixed = jnp.where(face % 2 == 0, 0, P_SIZE - 1)
    on_i = fixed * TR + major * P_SIZE + minor
    on_j = major * TR + fixed * P_SIZE + minor
    return (node == jnp.where(face < 2, on_i, on_j)).astype(bf16)


def left_half(shape):
    return lax.broadcasted_iota(jnp.int32, shape, len(shape) - 1) < TR


def read_wide(ref, index):
    return jnp.concatenate([ref[k, index, :] for k in range(ref.shape[0])], axis=1)


def write_wide(ref, index, value):
    for k in range(ref.shape[0]):
        ref[k, index, :] = value[:, k * LANES : (k + 1) * LANES]


def of_element(ref, e, elements):
    return pl.ds(e, ref.shape[1] // elements, stride=elements)


def store_traces(e, values, traces_ref):
    half = values.shape[0] // 2
    for pair in range(F // 2):
        a = values[:half, pair * LANES : (pair + 1) * LANES]
        b = values[half:, pair * LANES : (pair + 1) * LANES]
        left = left_half(a.shape)
        traces_ref[e * F + 2 * pair] = jnp.where(left, a, pltpu.roll(b, TR, 1)).astype(bf16)
        traces_ref[e * F + 2 * pair + 1] = jnp.where(left, pltpu.roll(a, TR, 1), b).astype(bf16)


def aligned(value, multiple):
    return value if isinstance(value, int) else pl.multiple_of(value, multiple)


def each(count, body, unroll=1):
    def step(i, carry):
        body(i)
        return carry

    if unroll >= count:
        for i in range(count):
            body(i)
        return
    lax.fori_loop(0, count, step, 0, unroll=unroll)


def each_tile(rows, tile, body):
    each(rows // tile, lambda i: body(pl.ds(aligned(i * tile, tile), tile)))


def pick_traces(lists_ref, traces_ref, sent_refs):
    for r, sent in enumerate(sent_refs):

        def body(j, r=r, sent=sent):
            sent[j] = traces_ref[lists_ref[r, j]]

        each(sent.shape[0], body)


def lifted_rows(e, refs_ref, traces_ref, arrived_refs):
    per = traces_ref.shape[0]
    slots = []
    for f in range(F):
        code = refs_ref[0, e * F + f]
        source, place = code // per, code % per
        value = jnp.where(source == 0, traces_ref[place].astype(f32), 0.0)
        for shift, arrived in enumerate(arrived_refs):
            here = source == shift + 1
            value = jnp.where(here, arrived[jnp.where(here, place, 0)].astype(f32), value)
        slots.append(value)
    tops, bottoms = [], []
    for pair in range(F // 2):
        a, b = slots[2 * pair], slots[2 * pair + 1]
        left = left_half(a.shape)
        tops.append(jnp.where(left, a, pltpu.roll(b, TR, 1)))
        bottoms.append(jnp.where(left, pltpu.roll(a, TR, 1), b))
    both = jnp.concatenate([jnp.concatenate(tops, 1), jnp.concatenate(bottoms, 1)], 0)
    return both.astype(bf16)


def opening_kernel(elements, unroll, start_ref, selector_ref, low_ref, high_ref, traces_ref, wide):
    rows = start_ref.shape[0]
    edge = low_ref.shape[0]
    low_ref[...] = start_ref[:edge]
    high_ref[...] = start_ref[rows - edge :]

    def widen(index):
        write_wide(wide, index, start_ref[index].astype(f32))

    each_tile(rows, ROW_TILE, widen)

    def element(e):
        own = read_wide(wide, of_element(wide, e, elements)).astype(bf16)
        store_traces(e, dot(own, selector_ref[...]), traces_ref)

    each(elements, element, unroll)


def picking_kernel(lists_ref, traces_ref, *sent_refs):
    pick_traces(lists_ref, traces_ref, sent_refs)


def paired(shards):
    return shards & (shards - 1) == 0


def asker_of(me, r, shards):
    return me ^ r if paired(shards) else lax.rem(me + r, shards)


def permute_of(asker, owner, shards):
    return asker ^ owner if paired(shards) else lax.rem(asker + shards - owner, shards)


def pattern_kernel(*refs):
    codes_refs, (me_ref, lists_ref, places_ref, level_ref) = refs[:-4], refs[-4:]
    shards = len(codes_refs)
    per = codes_refs[0].shape[0]
    every = shards * per
    me = me_ref[0]
    lane = lax.broadcasted_iota(jnp.int32, (per, every), 1)
    asked = [codes[:, :1] == lane for codes in codes_refs]
    need = jnp.concatenate(
        [jnp.max(a.astype(f32), axis=0, keepdims=True) for a in asked]
        + [jnp.zeros((8 - shards % 8, every), f32)] * (shards % 8 != 0),
        axis=0,
    ).astype(bf16)
    row = lax.broadcasted_iota(jnp.int32, (every, every), 0)
    column = lax.broadcasted_iota(jnp.int32, (every, every), 1)
    same = row // per == column // per
    before = (same & (row < column)).astype(bf16)
    rank = dot(need, before)
    total = dot(need, same.astype(bf16))
    over = (((0,), (1,)), ((), ()))
    rank_down = lax.dot_general(before, need, over, preferred_element_type=f32)
    need_down = lax.dot_general((row == column).astype(bf16), need, over, preferred_element_type=f32)
    owner = lax.broadcasted_iota(jnp.int32, total.shape, 1) // per
    number = lax.broadcasted_iota(jnp.int32, total.shape, 0)
    permute = permute_of(asker_of(me, number, shards), owner, shards)
    weighed = jnp.where(permute == 1, total * (1.0 / NEAR), total)
    weighed = jnp.where((permute == 0) | (number >= shards), 0.0, weighed)
    most = jnp.max(jnp.max(weighed, axis=1, keepdims=True), axis=0, keepdims=True)
    level = sum((most > cap).astype(jnp.int32) for cap in CAPS)
    level_ref[...] = jnp.broadcast_to(level, level_ref.shape)
    trace = lax.broadcasted_iota(jnp.int32, (every, LANES), 0)
    slot = lax.broadcasted_iota(jnp.int32, (every, LANES), 1)
    mine = trace // per == me
    lists_ref[...] = jnp.zeros_like(lists_ref)
    for r in range(1, shards):
        sent = mine & (need_down[:, r : r + 1] > 0.5) & (rank_down[:, r : r + 1].astype(jnp.int32) == slot)
        listed = jnp.sum(jnp.where(sent, (trace - me * per).astype(f32), 0.0), axis=0, keepdims=True)
        lists_ref[r - 1 : r, :] = listed.astype(jnp.int32)
    source = permute_of(me, lane // per, shards)
    place = jnp.where(source == 0, lane % per, rank[:1].astype(jnp.int32))
    code = jnp.where(asked[0], source * per + place, 0).astype(f32)
    found = jnp.sum(code, axis=1, keepdims=True)
    hit = jnp.sum(asked[0].astype(f32), axis=1, keepdims=True)
    found = jnp.where(hit > 0.5, found, float(every))
    down = lax.broadcasted_iota(jnp.int32, (per, LANES), 0)
    across = lax.broadcasted_iota(jnp.int32, (per, LANES), 1)
    turned = jnp.sum(jnp.where(down == across, jnp.broadcast_to(found, (per, LANES)), 0.0), axis=0, keepdims=True)
    places_ref[...] = turned.astype(jnp.int32)


def add_to(acc_ref, index, value):
    write_wide(acc_ref, index, read_wide(acc_ref, index) + value)


def near_kernel(step, layer, elements, unroll, *refs):
    if step == 2:
        here_ref, diag_ref, axial_ref, start_ref, acc_ref, wide = refs
    elif step == 3:
        here_ref, diag_ref, axial_ref, acc_ref, gram_ref, wide = refs
    else:
        here_ref, diag_ref, axial_ref, acc_ref, wide = refs
    rows, block = here_ref.shape
    tile = 2 * layer
    if step == 3:
        gram_ref[...] = jnp.zeros_like(gram_ref)

    def widen(i):
        index = pl.ds(aligned(i * tile, tile), tile)
        write_wide(wide, index, here_ref[index, :].astype(f32))

    each(rows // tile, widen)

    def element(e):
        index = of_element(wide, e, elements)
        own = read_wide(wide, index).astype(bf16)
        write_wide(acc_ref, index, dot(own, diag_ref[e]))
        if step == 3:
            gram_ref[...] += across(own, own)

    each(elements, element, unroll)

    layers = rows // layer
    for offset in [*range(-HW, 0), *range(1, HW + 1)]:
        if abs(offset) < layers:
            begin, end = max(0, -offset) * layer, (layers - max(0, offset)) * layer
            position = (offset + HW - (offset > 0)) * block
            values = here_ref[begin + offset * layer : end + offset * layer]
            add_to(acc_ref, slice(begin, end), dot(values, axial_ref[position : position + block]))

    if step != 3:

        def along(i):
            index = pl.ds(aligned(i * tile, tile), tile)
            total = read_wide(acc_ref, index) - shift_center * read_wide(wide, index)
            if step == 2:
                total -= (half_width / 2.0) * start_ref[index, :].astype(f32)
            write_wide(acc_ref, index, total)

        each(rows // tile, along)


def middle_kernel(layer, near_ref, low_ref, high_ref, axial_ref, acc_ref):
    del near_ref
    edge, block = low_ref.shape
    rows = acc_ref.shape[1]
    for reach in range(1, HW + 1):
        far = reach * layer
        below = dot(low_ref[edge - far :], axial_ref[(HW - reach) * block : (HW - reach + 1) * block])
        add_to(acc_ref, slice(0, far), below)
        above = dot(high_ref[:far], axial_ref[(HW + reach - 1) * block : (HW + reach) * block])
        add_to(acc_ref, slice(rows - far, rows), above)


def across(a, b):
    return lax.dot_general(a, b, (((1,), (1,)), ((), ())), preferred_element_type=f32)


def far_kernel(step, shards, elements, unroll, *refs):
    refs = list(refs)
    take = lambda n: [refs.pop(0) for _ in range(n)]
    places_ref, lists_ref, near_ref, traces_ref = take(4)
    arrived_refs = take(shards - 1)
    (face_ref,) = take(1)
    if step == 3:
        here_ref, gram_ref, out_ref, wide, projected = take(5)
        projected[...] = jnp.zeros_like(projected)

        def widen(index):
            write_wide(wide, index, here_ref[index, :].astype(f32))

        each_tile(here_ref.shape[0], ROW_TILE, widen)
    else:
        selector_ref, out_ref, out_low_ref, out_high_ref, out_traces_ref = take(5)
        sent_refs = take(shards - 1)
        (wide,) = take(1)
    scale = {1: 1.0 / half_width, 2: 2.0 / half_width, 3: 1.0}[step]

    def element(e):
        index = of_element(wide, e, elements)
        lifted = lifted_rows(e, places_ref, traces_ref, arrived_refs)
        total = (read_wide(near_ref, index) + dot(lifted, face_ref[e])) * scale
        if step == 3:
            own = read_wide(wide, index).astype(bf16)
            upper = total.astype(bf16)
            lower = (total - upper.astype(f32)).astype(bf16)
            projected[...] += across(own, upper) + across(own, lower)
            return
        new = total.astype(bf16)
        write_wide(wide, index, new.astype(f32))
        store_traces(e, dot(new, selector_ref[...]), out_traces_ref)

    each(elements, element, unroll)
    if step != 3:
        rows = out_ref.shape[0]
        edge = out_low_ref.shape[0]
        pick_traces(lists_ref, out_traces_ref, sent_refs)

        def narrow(index):
            out_ref[index, :] = read_wide(wide, index).astype(bf16)

        each_tile(rows, ROW_TILE, narrow)
        out_low_ref[...] = out_ref[:edge]
        out_high_ref[...] = out_ref[rows - edge :]
        return

    size = projected.shape[0]
    vectors = out_ref.shape[0] // 2
    down = lax.broadcasted_iota(jnp.int32, (size, size), 0)
    over = lax.broadcasted_iota(jnp.int32, (size, size), 1)
    keep = down // vectors == over // vectors
    group = (
        lax.broadcasted_iota(jnp.int32, (size, LANES), 0) % vectors
        == lax.broadcasted_iota(jnp.int32, (size, LANES), 1)
    ).astype(f32)
    for place, ref in enumerate((gram_ref, projected)):
        value = jnp.where(keep, ref[...], 0.0).reshape(size // vectors, vectors, size).sum(0)
        value = jnp.dot(value, group, precision=lax.Precision.HIGHEST, preferred_element_type=f32)
        out_ref[place * vectors : (place + 1) * vectors] = value


def shape(dims, dtype=bf16):
    return jax.ShapeDtypeStruct(dims, dtype)


def params(rows):
    return pltpu.CompilerParams(vmem_limit_bytes=14 * 2**20 + rows * 12 * 2**10)


def rotate(value, axis, shift):
    count = lax.axis_size(axis)
    return lax.ppermute(value, axis, [(i, (i + shift) % count) for i in range(count)])


def send_traces(value, r):
    count = lax.axis_size("xs")
    if paired(count):
        return lax.ppermute(value, "xs", [(i, i ^ r) for i in range(count)])
    return rotate(value, "xs", r)


def add_over(value, axis):
    count = lax.axis_size(axis)
    if not paired(count):
        return lax.psum(value, axis)
    step = 1
    while step < count:
        far = lambda distance: lax.ppermute(value, axis, [(i, i ^ distance) for i in range(count)])
        if (count // step).bit_length() % 2 == 0:
            value = value + far(step)
            step *= 2
        else:
            value = (value + far(step)) + (far(2 * step) + far(3 * step))
            step *= 4
    return value


def local(start_vectors, diag_blocks, face_blocks, axial_blocks, neighbor_ids, neighbor_face, face_mask):
    layers, vectors, elements, block = start_vectors.shape
    shards = lax.axis_size("xs")
    me = lax.axis_index("xs").astype(jnp.int32)
    per = elements * F
    layer = vectors * elements
    rows = layers * layer
    edge = HW * layer
    half = layers * vectors // 2
    wide_rows = (block // LANES, rows, LANES)
    face_flat = face_blocks.reshape(elements, F * TR, block)
    axial_flat = axial_blocks.reshape(2 * HW * block, block)
    selector = trace_selector(block)

    codes = jnp.where(face_mask == 1, neighbor_ids * F + neighbor_face, -1).reshape(per, 1)
    codes = jnp.broadcast_to(codes, (per, LANES)).astype(jnp.int32)
    back = lambda r: send_traces(codes, r if paired(shards) else shards - r)
    all_codes = [codes] + [back(r) for r in range(1, shards)]
    lists, places, level = pl.pallas_call(
        pattern_kernel,
        out_shape=[shape((8, LANES), jnp.int32), shape((1, LANES), jnp.int32), shape((1, LANES), jnp.int32)],
        in_specs=[VMEM] * shards + [SMEM],
        out_specs=[VMEM] * 3,
        compiler_params=params(rows),
        name="pattern",
    )(*all_codes, me.reshape(1))

    start_flat = start_vectors.reshape(rows, block)
    low, high, traces = pl.pallas_call(
        functools.partial(opening_kernel, elements, UNROLL),
        out_shape=[shape((edge, block)), shape((edge, block)), shape((per, half, LANES))],
        in_specs=[VMEM] * 2,
        out_specs=[VMEM] * 3,
        scratch_shapes=[pltpu.VMEM(wide_rows, f32)],
        compiler_params=params(rows),
        name="opening",
    )(start_flat, selector)

    def one_round(step, caps, here, low, high, traces, sent):
        unroll = 1 if min(caps) == per else UNROLL
        arrived = [send_traces(s, r + 1) for r, s in enumerate(sent)]
        from_low = rotate(high, "pipe", 1)
        from_high = rotate(low, "pipe", -1)
        size = layers * vectors
        operands = [here, diag_blocks, axial_flat] + [start_flat] * (step == 2)
        outs = [shape(wide_rows, f32)] + [shape((size, size), f32)] * (step == 3)
        near, *gram = pl.pallas_call(
            functools.partial(near_kernel, step, layer, elements, unroll),
            out_shape=outs,
            in_specs=[VMEM] * len(operands),
            out_specs=[VMEM] * len(outs),
            scratch_shapes=[pltpu.VMEM(wide_rows, f32)],
            compiler_params=params(rows),
            cost_estimate=pl.CostEstimate(flops=14 * rows * block * block, bytes_accessed=10**7, transcendentals=0),
            name=f"near_{step}",
        )(*operands)
        near = pl.pallas_call(
            functools.partial(middle_kernel, layer),
            out_shape=shape(wide_rows, f32),
            in_specs=[VMEM] * 4,
            out_specs=VMEM,
            input_output_aliases={0: 0},
            compiler_params=params(rows),
            cost_estimate=pl.CostEstimate(flops=5 * rows * block * block, bytes_accessed=10**7, transcendentals=0),
            name=f"middle_{step}",
        )(near, from_low, from_high, axial_flat)
        operands = [places, lists, near, traces, *arrived, face_flat]
        scratch = [pltpu.VMEM(wide_rows, f32)]
        if step == 3:
            operands += [here, *gram]
            outs = [shape((2 * vectors, LANES), f32)]
            scratch += [pltpu.VMEM((size, size), f32)]
        else:
            operands += [selector]
            outs = [shape((rows, block)), shape((edge, block)), shape((edge, block)), shape((per, half, LANES))]
            outs += [shape((cap, half, LANES)) for cap in caps]
        return pl.pallas_call(
            functools.partial(far_kernel, step, shards, elements, unroll),
            out_shape=outs,
            in_specs=[SMEM] * 2 + [VMEM] * (len(operands) - 2),
            out_specs=[VMEM] * len(outs),
            scratch_shapes=scratch,
            compiler_params=params(rows),
            cost_estimate=pl.CostEstimate(flops=2 * rows * block * block, bytes_accessed=10**7, transcendentals=0),
            name=f"far_{step}",
        )(*operands)

    def run(cap):
        caps = [min(per, cap * NEAR if r == 0 else cap) for r in range(shards - 1)]
        sent = pl.pallas_call(
            picking_kernel,
            out_shape=[shape((cap, half, LANES)) for cap in caps],
            in_specs=[SMEM, VMEM],
            out_specs=[VMEM] * (shards - 1),
            compiler_params=params(rows),
            name="picking",
        )(lists, traces)
        first, *rest = one_round(1, caps, start_flat, low, high, traces, sent)
        filtered, *rest = one_round(2, caps, first, rest[0], rest[1], rest[2], rest[3:])
        (both,) = one_round(3, caps, filtered, rest[0], rest[1], rest[2], rest[3:])
        return filtered, both

    branches = [functools.partial(run, cap) for cap in (*CAPS, per)]
    filtered, both = lax.switch(level[0, 0], branches)
    both = add_over(add_over(both, "pipe"), "xs")
    count_all = float(layers * lax.axis_size("pipe") * elements * shards * block)
    both = both[:, :vectors] / count_all
    return filtered.reshape(start_vectors.shape), both[:vectors], both[vectors:]


def solution(mesh):
    in_specs = (
        P("pipe", None, "xs", None),
        P("xs", None, None),
        P("xs", None, None, None),
        P(),
        P("xs", None),
        P("xs", None),
        P("xs", None),
    )
    out_specs = (P("pipe", None, "xs", None), P(), P())
    return jax.shard_map(local, mesh=mesh, in_specs=in_specs, out_specs=out_specs, check_vma=False)
```

```python
import functools

import jax
import jax.numpy as jnp
from jax import lax
from jax.experimental import pallas as pl
from jax.experimental.pallas import tpu as pltpu
from jax.sharding import PartitionSpec as P

P_SIZE = 8
F = 4
HW = 4
TR = P_SIZE * P_SIZE
LANES = 128
CAPS = (9, 12)
ROW_TILE = 256
UNROLL = 4
MORE = 3

shift_center = 0.3
half_width = 1.2

VMEM = pl.BlockSpec(memory_space=pltpu.VMEM)
SMEM = pl.BlockSpec(memory_space=pltpu.SMEM)
ANY = pl.BlockSpec(memory_space=pl.ANY)
bf16 = jnp.bfloat16
f32 = jnp.float32


def dot(a, b):
    return jnp.dot(a, b, preferred_element_type=f32)


def trace_selector(block):
    node = lax.broadcasted_iota(jnp.int32, (block, F * TR), 0)
    column = lax.broadcasted_iota(jnp.int32, (block, F * TR), 1)
    face, entry = column // TR, column % TR
    major, minor = entry // P_SIZE, entry % P_SIZE
    fixed = jnp.where(face % 2 == 0, 0, P_SIZE - 1)
    on_i = fixed * TR + major * P_SIZE + minor
    on_j = major * TR + fixed * P_SIZE + minor
    return (node == jnp.where(face < 2, on_i, on_j)).astype(bf16)


def left_half(shape):
    return lax.broadcasted_iota(jnp.int32, shape, len(shape) - 1) < TR


def read_wide(ref, index):
    return jnp.concatenate([ref[k, index, :] for k in range(ref.shape[0])], axis=1)


def write_wide(ref, index, value):
    for k in range(ref.shape[0]):
        ref[k, index, :] = value[:, k * LANES : (k + 1) * LANES]


def of_element(ref, e, elements):
    return pl.ds(e, ref.shape[1] // elements, stride=elements)


def store_traces(e, values, traces_ref):
    half = values.shape[0] // 2
    for pair in range(F // 2):
        a = values[:half, pair * LANES : (pair + 1) * LANES]
        b = values[half:, pair * LANES : (pair + 1) * LANES]
        left = left_half(a.shape)
        traces_ref[e * F + 2 * pair] = jnp.where(left, a, pltpu.roll(b, TR, 1)).astype(bf16)
        traces_ref[e * F + 2 * pair + 1] = jnp.where(left, pltpu.roll(a, TR, 1), b).astype(bf16)


def aligned(value, multiple):
    return value if isinstance(value, int) else pl.multiple_of(value, multiple)


def each(count, body, unroll=1):
    def step(i, carry):
        body(i)
        return carry

    if unroll >= count:
        for i in range(count):
            body(i)
        return
    lax.fori_loop(0, count, step, 0, unroll=unroll)


def each_tile(rows, tile, body):
    each(rows // tile, lambda i: body(pl.ds(aligned(i * tile, tile), tile)))


def pick_traces(lists_ref, traces_ref, sent_refs):
    for r, sent in enumerate(sent_refs):

        def body(j, r=r, sent=sent):
            sent[j] = traces_ref[lists_ref[r, j]]

        each(sent.shape[0], body)


def lifted_rows(e, refs_ref, traces_ref, arrived_refs):
    per = traces_ref.shape[0]
    slots = []
    for f in range(F):
        code = refs_ref[0, e * F + f]
        source, place = code // per, code % per
        value = jnp.where(source == 0, traces_ref[place].astype(f32), 0.0)
        for shift, arrived in enumerate(arrived_refs):
            here = source == shift + 1
            value = jnp.where(here, arrived[jnp.where(here, place, 0)].astype(f32), value)
        slots.append(value)
    tops, bottoms = [], []
    for pair in range(F // 2):
        a, b = slots[2 * pair], slots[2 * pair + 1]
        left = left_half(a.shape)
        tops.append(jnp.where(left, a, pltpu.roll(b, TR, 1)))
        bottoms.append(jnp.where(left, pltpu.roll(a, TR, 1), b))
    both = jnp.concatenate([jnp.concatenate(tops, 1), jnp.concatenate(bottoms, 1)], 0)
    return both.astype(bf16)


def opening_kernel(elements, unroll, start_ref, selector_ref, low_ref, high_ref, traces_ref, wide):
    rows = start_ref.shape[0]
    edge = low_ref.shape[0]

    def chosen(index):
        write_wide(wide, index, dot(start_ref[index, :], selector_ref[...]))

    each_tile(rows, ROW_TILE, chosen)
    each(elements, lambda e: store_traces(e, read_wide(wide, of_element(wide, e, elements)), traces_ref), unroll)
    low_ref[...] = start_ref[:edge]
    high_ref[...] = start_ref[rows - edge :]


def picking_kernel(lists_ref, traces_ref, *sent_refs):
    pick_traces(lists_ref, traces_ref, sent_refs)


def paired(shards):
    return shards & (shards - 1) == 0


def asker_of(me, r, shards):
    return me ^ r if paired(shards) else lax.rem(me + r, shards)


def permute_of(asker, owner, shards):
    return asker ^ owner if paired(shards) else lax.rem(asker + shards - owner, shards)


def pattern_kernel(*refs):
    codes_refs, (me_ref, lists_ref, places_ref, level_ref) = refs[:-4], refs[-4:]
    shards = len(codes_refs)
    per = codes_refs[0].shape[0]
    every = shards * per
    me = me_ref[0]
    lane = lax.broadcasted_iota(jnp.int32, (per, every), 1)
    asked = [codes[:, :1] == lane for codes in codes_refs]
    need = jnp.concatenate(
        [jnp.max(a.astype(f32), axis=0, keepdims=True) for a in asked]
        + [jnp.zeros((8 - shards % 8, every), f32)] * (shards % 8 != 0),
        axis=0,
    ).astype(bf16)
    row = lax.broadcasted_iota(jnp.int32, (every, every), 0)
    column = lax.broadcasted_iota(jnp.int32, (every, every), 1)
    same = row // per == column // per
    before = (same & (row < column)).astype(bf16)
    rank = dot(need, before)
    total = dot(need, same.astype(bf16))
    over = (((0,), (1,)), ((), ()))
    rank_down = lax.dot_general(before, need, over, preferred_element_type=f32)
    need_down = lax.dot_general((row == column).astype(bf16), need, over, preferred_element_type=f32)
    owner = lax.broadcasted_iota(jnp.int32, total.shape, 1) // per
    number = lax.broadcasted_iota(jnp.int32, total.shape, 0)
    permute = permute_of(asker_of(me, number, shards), owner, shards)
    weighed = jnp.where(permute == 1, total - MORE, total)
    weighed = jnp.where((permute == 0) | (number >= shards), 0.0, weighed)
    most = jnp.max(jnp.max(weighed, axis=1, keepdims=True), axis=0, keepdims=True)
    level = sum((most > cap).astype(jnp.int32) for cap in CAPS)
    level_ref[...] = jnp.broadcast_to(level, level_ref.shape)
    trace = lax.broadcasted_iota(jnp.int32, (every, LANES), 0)
    slot = lax.broadcasted_iota(jnp.int32, (every, LANES), 1)
    mine = trace // per == me
    lists_ref[...] = jnp.zeros_like(lists_ref)
    for r in range(1, shards):
        sent = mine & (need_down[:, r : r + 1] > 0.5) & (rank_down[:, r : r + 1].astype(jnp.int32) == slot)
        listed = jnp.sum(jnp.where(sent, (trace - me * per).astype(f32), 0.0), axis=0, keepdims=True)
        lists_ref[r - 1 : r, :] = listed.astype(jnp.int32)
    source = permute_of(me, lane // per, shards)
    place = jnp.where(source == 0, lane % per, rank[:1].astype(jnp.int32))
    code = jnp.where(asked[0], source * per + place, 0).astype(f32)
    found = jnp.sum(code, axis=1, keepdims=True)
    hit = jnp.sum(asked[0].astype(f32), axis=1, keepdims=True)
    found = jnp.where(hit > 0.5, found, float(every))
    down = lax.broadcasted_iota(jnp.int32, (per, LANES), 0)
    across = lax.broadcasted_iota(jnp.int32, (per, LANES), 1)
    turned = jnp.sum(jnp.where(down == across, jnp.broadcast_to(found, (per, LANES)), 0.0), axis=0, keepdims=True)
    places_ref[...] = turned.astype(jnp.int32)


def add_to(acc_ref, index, value):
    write_wide(acc_ref, index, read_wide(acc_ref, index) + value)


def near_kernel(step, layer, elements, unroll, *refs):
    if step == 2:
        here_ref, diag_ref, axial_ref, start_ref, acc_ref, wide, ext = refs
    elif step == 3:
        here_ref, diag_ref, axial_ref, acc_ref, gram_ref, own_ref, copy_ref, wide, ext = refs
        copy_ref[...] = here_ref[...]
    else:
        here_ref, diag_ref, axial_ref, acc_ref, wide, ext = refs
    rows, block = here_ref.shape
    tile = 2 * layer
    if step == 3:
        gram_ref[...] = jnp.zeros_like(gram_ref)

    def widen(i):
        index = pl.ds(aligned(i * tile, tile), tile)
        write_wide(wide, index, here_ref[index, :].astype(f32))

    each(rows // tile, widen)

    def element(e):
        index = of_element(wide, e, elements)
        own = read_wide(wide, index).astype(bf16)
        write_wide(acc_ref, index, dot(own, diag_ref[e]))
        if step == 3:
            gram_ref[...] += across(own, own)
            own_ref[e] = own

    each(elements, element, unroll)

    if unroll > 1:
        layers = rows // layer
        for offset in [*range(-HW, 0), *range(1, HW + 1)]:
            if abs(offset) < layers:
                begin, end = max(0, -offset) * layer, (layers - max(0, offset)) * layer
                position = (offset + HW - (offset > 0)) * block
                values = here_ref[begin + offset * layer : end + offset * layer]
                add_to(acc_ref, slice(begin, end), dot(values, axial_ref[position : position + block]))
    else:
        edge = HW * layer
        ext[:edge] = jnp.zeros((edge, block), bf16)
        ext[edge : edge + rows] = here_ref[...]
        ext[edge + rows :] = jnp.zeros((edge, block), bf16)

        def offset(p):
            begin = (p + jnp.where(p < HW, 0, 1)) * layer
            weights = axial_ref[pl.ds(aligned(p * block, block), block), :]

            def part(i):
                base = aligned(i * tile, tile)
                values = ext[pl.ds(aligned(begin + base, layer), tile), :]
                add_to(acc_ref, pl.ds(base, tile), dot(values, weights))

            each(rows // tile, part)

        each(2 * HW, offset)

    if step != 3:

        def along(i):
            index = pl.ds(aligned(i * tile, tile), tile)
            total = read_wide(acc_ref, index) - shift_center * read_wide(wide, index)
            if step == 2:
                total -= (half_width / 2.0) * start_ref[index, :].astype(f32)
            write_wide(acc_ref, index, total)

        each(rows // tile, along)


def middle_kernel(layer, near_ref, low_ref, high_ref, axial_ref, acc_ref):
    del near_ref
    edge, block = low_ref.shape
    rows = acc_ref.shape[1]
    for reach in range(1, HW + 1):
        far = reach * layer
        below = dot(low_ref[edge - far :], axial_ref[(HW - reach) * block : (HW - reach + 1) * block])
        add_to(acc_ref, slice(0, far), below)
        above = dot(high_ref[:far], axial_ref[(HW + reach - 1) * block : (HW + reach) * block])
        add_to(acc_ref, slice(rows - far, rows), above)


def across(a, b):
    return lax.dot_general(a, b, (((1,), (1,)), ((), ())), preferred_element_type=f32)


def far_kernel(step, shards, elements, unroll, *refs):
    refs = list(refs)
    take = lambda n: [refs.pop(0) for _ in range(n)]
    places_ref, lists_ref, near_ref, traces_ref = take(4)
    arrived_refs = take(shards - 1)
    (face_ref,) = take(1)
    if step == 3:
        own_ref, gram_ref, out_ref, projected = take(4)
        projected[...] = jnp.zeros_like(projected)
    else:
        selector_ref, out_ref, out_low_ref, out_high_ref, out_traces_ref = take(5)
        sent_refs = take(shards - 1)
        (wide,) = take(1)
    scale = {1: 1.0 / half_width, 2: 2.0 / half_width, 3: 1.0}[step]

    def element(e):
        index = of_element(near_ref, e, elements)
        lifted = lifted_rows(e, places_ref, traces_ref, arrived_refs)
        total = (read_wide(near_ref, index) + dot(lifted, face_ref[e])) * scale
        if step == 3:
            own = own_ref[e]
            upper = total.astype(bf16)
            lower = (total - upper.astype(f32)).astype(bf16)
            projected[...] += across(own, upper) + across(own, lower)
            return
        new = total.astype(bf16)
        write_wide(wide, index, new.astype(f32))
        store_traces(e, dot(new, selector_ref[...]), out_traces_ref)

    each(elements, element, unroll)
    if step != 3:
        rows = out_ref.shape[0]
        edge = out_low_ref.shape[0]
        pick_traces(lists_ref, out_traces_ref, sent_refs)

        def narrow(index):
            out_ref[index, :] = read_wide(wide, index).astype(bf16)

        each_tile(rows, ROW_TILE, narrow)
        out_low_ref[...] = out_ref[:edge]
        out_high_ref[...] = out_ref[rows - edge :]
        return

    size = projected.shape[0]
    vectors = out_ref.shape[0] // 2
    down = lax.broadcasted_iota(jnp.int32, (size, size), 0)
    over = lax.broadcasted_iota(jnp.int32, (size, size), 1)
    keep = down // vectors == over // vectors
    group = (
        lax.broadcasted_iota(jnp.int32, (size, LANES), 0) % vectors
        == lax.broadcasted_iota(jnp.int32, (size, LANES), 1)
    ).astype(f32)
    for place, ref in enumerate((gram_ref, projected)):
        value = jnp.where(keep, ref[...], 0.0).reshape(size // vectors, vectors, size).sum(0)
        value = jnp.dot(value, group, precision=lax.Precision.HIGHEST, preferred_element_type=f32)
        out_ref[place * vectors : (place + 1) * vectors] = value


def shape(dims, dtype=bf16):
    return jax.ShapeDtypeStruct(dims, dtype)


def params(rows):
    return pltpu.CompilerParams(vmem_limit_bytes=14 * 2**20 + rows * 12 * 2**10)


def rotate(value, axis, shift):
    count = lax.axis_size(axis)
    return lax.ppermute(value, axis, [(i, (i + shift) % count) for i in range(count)])


def send_traces(value, r):
    count = lax.axis_size("xs")
    if paired(count):
        return lax.ppermute(value, "xs", [(i, i ^ r) for i in range(count)])
    return rotate(value, "xs", r)


def add_over(value, axis):
    count = lax.axis_size(axis)
    if not paired(count):
        return lax.psum(value, axis)
    step = 1
    while step < count:
        far = lambda distance: lax.ppermute(value, axis, [(i, i ^ distance) for i in range(count)])
        if (count // step).bit_length() % 2 == 0:
            value = value + far(step)
            step *= 2
        else:
            value = (value + far(step)) + (far(2 * step) + far(3 * step))
            step *= 4
    return value


def local(start_vectors, diag_blocks, face_blocks, axial_blocks, neighbor_ids, neighbor_face, face_mask):
    layers, vectors, elements, block = start_vectors.shape
    shards = lax.axis_size("xs")
    me = lax.axis_index("xs").astype(jnp.int32)
    per = elements * F
    layer = vectors * elements
    rows = layers * layer
    edge = HW * layer
    half = layers * vectors // 2
    wide_rows = (block // LANES, rows, LANES)
    face_flat = face_blocks.reshape(elements, F * TR, block)
    axial_flat = axial_blocks.reshape(2 * HW * block, block)
    selector = trace_selector(block)

    codes = jnp.where(face_mask == 1, neighbor_ids * F + neighbor_face, -1).reshape(per, 1)
    codes = jnp.broadcast_to(codes, (per, LANES)).astype(jnp.int32)
    back = lambda r: send_traces(codes, r if paired(shards) else shards - r)
    all_codes = [codes] + [back(r) for r in range(1, shards)]
    lists, places, level = pl.pallas_call(
        pattern_kernel,
        out_shape=[shape((8, LANES), jnp.int32), shape((1, LANES), jnp.int32), shape((1, LANES), jnp.int32)],
        in_specs=[VMEM] * shards + [SMEM],
        out_specs=[VMEM] * 3,
        compiler_params=params(rows),
        name="pattern",
    )(*all_codes, me.reshape(1))

    start_flat = start_vectors.reshape(rows, block)
    low, high, traces = pl.pallas_call(
        functools.partial(opening_kernel, elements, UNROLL),
        out_shape=[shape((edge, block)), shape((edge, block)), shape((per, half, LANES))],
        in_specs=[VMEM] * 2,
        out_specs=[VMEM] * 3,
        scratch_shapes=[pltpu.VMEM((F * TR // LANES, rows, LANES), f32)],
        compiler_params=params(rows),
        name="opening",
    )(start_flat, selector)

    def one_round(step, caps, here, low, high, traces, sent):
        unroll = UNROLL if caps[-1] == CAPS[0] else 1
        busy = 1 if caps[-1] == per else UNROLL
        arrived = [send_traces(s, r + 1) for r, s in enumerate(sent)]
        from_low = rotate(high, "pipe", 1)
        from_high = rotate(low, "pipe", -1)
        size = layers * vectors
        operands = [here, diag_blocks, axial_flat] + [start_flat] * (step == 2)
        outs = [shape(wide_rows, f32)]
        if step == 3:
            outs += [shape((size, size), f32), shape((elements, size, block)), shape((rows, block))]
        near, *extra = pl.pallas_call(
            functools.partial(near_kernel, step, layer, elements, unroll),
            out_shape=outs,
            in_specs=[VMEM] * len(operands),
            out_specs=[VMEM] * len(outs),
            scratch_shapes=[
                pltpu.VMEM(wide_rows, f32),
                pltpu.VMEM((rows + 2 * edge if unroll == 1 else 16, block), bf16),
            ],
            compiler_params=params(rows),
            cost_estimate=pl.CostEstimate(flops=14 * rows * block * block, bytes_accessed=10**7, transcendentals=0),
            name=f"near_{step}",
        )(*operands)
        near = pl.pallas_call(
            functools.partial(middle_kernel, layer),
            out_shape=shape(wide_rows, f32),
            in_specs=[VMEM] * 4,
            out_specs=VMEM,
            input_output_aliases={0: 0},
            compiler_params=params(rows),
            cost_estimate=pl.CostEstimate(flops=5 * rows * block * block, bytes_accessed=10**7, transcendentals=0),
            name=f"middle_{step}",
        )(near, from_low, from_high, axial_flat)
        operands = [places, lists, near, traces, *arrived, face_flat]
        if step == 3:
            operands += [extra[1], extra[0]]
            outs = [shape((2 * vectors, LANES), f32)]
            scratch = [pltpu.VMEM((size, size), f32)]
        else:
            scratch = [pltpu.VMEM(wide_rows, f32)]
            operands += [selector]
            outs = [shape((rows, block)), shape((edge, block)), shape((edge, block)), shape((per, half, LANES))]
            outs += [shape((cap, half, LANES)) for cap in caps]
        results = pl.pallas_call(
            functools.partial(far_kernel, step, shards, elements, busy),
            out_shape=outs,
            in_specs=[SMEM] * 2 + [VMEM] * (len(operands) - 2),
            out_specs=[VMEM] * len(outs),
            scratch_shapes=scratch,
            compiler_params=params(rows),
            cost_estimate=pl.CostEstimate(flops=2 * rows * block * block, bytes_accessed=10**7, transcendentals=0),
            name=f"far_{step}",
        )(*operands)
        return [extra[2], *results] if step == 3 else results

    def run(cap):
        caps = [min(per, cap + MORE if r == 0 else cap) for r in range(shards - 1)]
        sent = pl.pallas_call(
            picking_kernel,
            out_shape=[shape((cap, half, LANES)) for cap in caps],
            in_specs=[SMEM, VMEM],
            out_specs=[VMEM] * (shards - 1),
            compiler_params=params(rows),
            name="picking",
        )(lists, traces)
        first, *rest = one_round(1, caps, start_flat, low, high, traces, sent)
        second, *rest = one_round(2, caps, first, rest[0], rest[1], rest[2], rest[3:])
        filtered, both = one_round(3, caps, second, rest[0], rest[1], rest[2], rest[3:])
        return filtered, both

    branches = [functools.partial(run, cap) for cap in (*CAPS, per)]
    filtered, both = lax.switch(level[0, 0], branches)
    both = add_over(add_over(both, "pipe"), "xs")
    count_all = float(layers * lax.axis_size("pipe") * elements * shards * block)
    both = both[:, :vectors] / count_all
    return filtered.reshape(start_vectors.shape), both[:vectors], both[vectors:]


def solution(mesh):
    in_specs = (
        P("pipe", None, "xs", None),
        P("xs", None, None),
        P("xs", None, None, None),
        P(),
        P("xs", None),
        P("xs", None),
        P("xs", None),
    )
    out_specs = (P("pipe", None, "xs", None), P(), P())
    return jax.shard_map(local, mesh=mesh, in_specs=in_specs, out_specs=out_specs, check_vma=False)
```

```python
import functools

import jax
import jax.numpy as jnp
from jax import lax
from jax.experimental import pallas as pl
from jax.experimental.pallas import tpu as pltpu
from jax.sharding import PartitionSpec as P

P_SIZE = 8
F = 4
HW = 4
TR = P_SIZE * P_SIZE
LANES = 128
CAPS = (9, 12)
ROW_TILE = 256
UNROLL = 8
MORE = 3

shift_center = 0.3
half_width = 1.2

VMEM = pl.BlockSpec(memory_space=pltpu.VMEM)
SMEM = pl.BlockSpec(memory_space=pltpu.SMEM)
ANY = pl.BlockSpec(memory_space=pl.ANY)
bf16 = jnp.bfloat16
f32 = jnp.float32


def dot(a, b):
    return jnp.dot(a, b, preferred_element_type=f32)


def trace_selector(block):
    node = lax.broadcasted_iota(jnp.int32, (block, F * TR), 0)
    column = lax.broadcasted_iota(jnp.int32, (block, F * TR), 1)
    face, entry = column // TR, column % TR
    major, minor = entry // P_SIZE, entry % P_SIZE
    fixed = jnp.where(face % 2 == 0, 0, P_SIZE - 1)
    on_i = fixed * TR + major * P_SIZE + minor
    on_j = major * TR + fixed * P_SIZE + minor
    return (node == jnp.where(face < 2, on_i, on_j)).astype(bf16)


def left_half(shape):
    return lax.broadcasted_iota(jnp.int32, shape, len(shape) - 1) < TR


def read_wide(ref, index):
    return jnp.concatenate([ref[k, index, :] for k in range(ref.shape[0])], axis=1)


def write_wide(ref, index, value):
    for k in range(ref.shape[0]):
        ref[k, index, :] = value[:, k * LANES : (k + 1) * LANES]


def of_element(ref, e, elements):
    return pl.ds(e, ref.shape[1] // elements, stride=elements)


def store_traces(e, values, traces_ref):
    half = values.shape[0] // 2
    for pair in range(F // 2):
        a = values[:half, pair * LANES : (pair + 1) * LANES]
        b = values[half:, pair * LANES : (pair + 1) * LANES]
        left = left_half(a.shape)
        traces_ref[e * F + 2 * pair] = jnp.where(left, a, pltpu.roll(b, TR, 1)).astype(bf16)
        traces_ref[e * F + 2 * pair + 1] = jnp.where(left, pltpu.roll(a, TR, 1), b).astype(bf16)


def aligned(value, multiple):
    return value if isinstance(value, int) else pl.multiple_of(value, multiple)


def each(count, body, unroll=1):
    def step(i, carry):
        body(i)
        return carry

    if unroll >= count:
        for i in range(count):
            body(i)
        return
    lax.fori_loop(0, count, step, 0, unroll=unroll)


def each_tile(rows, tile, body):
    each(rows // tile, lambda i: body(pl.ds(aligned(i * tile, tile), tile)))


def pick_traces(lists_ref, traces_ref, sent_refs, unroll):
    for r, sent in enumerate(sent_refs):

        def body(j, r=r, sent=sent):
            sent[j] = traces_ref[lists_ref[r, j]]

        each(sent.shape[0], body, sent.shape[0] if unroll > 1 else 1)


def lifted_rows(e, refs_ref, traces_ref, arrived_refs):
    per = traces_ref.shape[0]
    slots = []
    for f in range(F):
        code = refs_ref[0, e * F + f]
        source, place = code // per, code % per
        value = jnp.where(source == 0, traces_ref[place].astype(f32), 0.0)
        for shift, arrived in enumerate(arrived_refs):
            here = source == shift + 1
            value = jnp.where(here, arrived[jnp.where(here, place, 0)].astype(f32), value)
        slots.append(value)
    tops, bottoms = [], []
    for pair in range(F // 2):
        a, b = slots[2 * pair], slots[2 * pair + 1]
        left = left_half(a.shape)
        tops.append(jnp.where(left, a, pltpu.roll(b, TR, 1)))
        bottoms.append(jnp.where(left, pltpu.roll(a, TR, 1), b))
    both = jnp.concatenate([jnp.concatenate(tops, 1), jnp.concatenate(bottoms, 1)], 0)
    return both.astype(bf16)


def keep_rows(e, new, out_ref, low_ref, high_ref):
    edge = low_ref.shape[1]
    out_ref[e] = new
    low_ref[e] = new[:edge]
    high_ref[e] = new[new.shape[0] - edge :]


def opening_kernel(elements, start_hbm, selector_ref, out_ref, low_ref, high_ref, traces_ref, begun, wide, sems):
    parts = sems.shape[0]
    tile = begun.shape[0] // parts
    loads = []
    for i in range(parts):
        index = pl.ds(i * tile, tile)
        loads.append(pltpu.make_async_copy(start_hbm.at[index], begun.at[index], sems.at[i]))
        loads[-1].start()
    for i, load in enumerate(loads):
        load.wait()
        index = pl.ds(i * tile, tile)
        write_wide(wide, index, begun[index, :].astype(f32))

    def element(e):
        own = read_wide(wide, of_element(wide, e, elements)).astype(bf16)
        keep_rows(e, own, out_ref, low_ref, high_ref)
        store_traces(e, dot(own, selector_ref[...]), traces_ref)

    each(elements, element, elements)


def picking_kernel(unroll, lists_ref, traces_ref, *sent_refs):
    pick_traces(lists_ref, traces_ref, sent_refs, unroll)


def paired(shards):
    return shards & (shards - 1) == 0


def asker_of(me, r, shards):
    return me ^ r if paired(shards) else lax.rem(me + r, shards)


def permute_of(asker, owner, shards):
    return asker ^ owner if paired(shards) else lax.rem(asker + shards - owner, shards)


def pattern_kernel(*refs):
    codes_refs, (me_ref, lists_ref, places_ref, level_ref) = refs[:-4], refs[-4:]
    shards = len(codes_refs)
    per = codes_refs[0].shape[0]
    every = shards * per
    me = me_ref[0]
    lane = lax.broadcasted_iota(jnp.int32, (per, every), 1)
    asked = [codes[:, :1] == lane for codes in codes_refs]
    need = jnp.concatenate(
        [jnp.max(a.astype(f32), axis=0, keepdims=True) for a in asked]
        + [jnp.zeros((8 - shards % 8, every), f32)] * (shards % 8 != 0),
        axis=0,
    ).astype(bf16)
    row = lax.broadcasted_iota(jnp.int32, (every, every), 0)
    column = lax.broadcasted_iota(jnp.int32, (every, every), 1)
    same = row // per == column // per
    before = (same & (row < column)).astype(bf16)
    rank = dot(need, before)
    total = dot(need, same.astype(bf16))
    over = (((0,), (1,)), ((), ()))
    rank_down = lax.dot_general(before, need, over, preferred_element_type=f32)
    need_down = lax.dot_general((row == column).astype(bf16), need, over, preferred_element_type=f32)
    owner = lax.broadcasted_iota(jnp.int32, total.shape, 1) // per
    number = lax.broadcasted_iota(jnp.int32, total.shape, 0)
    permute = permute_of(asker_of(me, number, shards), owner, shards)
    weighed = jnp.where(permute == 1, total - MORE, total)
    weighed = jnp.where((permute == 0) | (number >= shards), 0.0, weighed)
    most = jnp.max(jnp.max(weighed, axis=1, keepdims=True), axis=0, keepdims=True)
    level = sum((most > cap).astype(jnp.int32) for cap in CAPS)
    level_ref[...] = jnp.broadcast_to(level, level_ref.shape)
    trace = lax.broadcasted_iota(jnp.int32, (every, LANES), 0)
    slot = lax.broadcasted_iota(jnp.int32, (every, LANES), 1)
    mine = trace // per == me
    lists_ref[...] = jnp.zeros_like(lists_ref)
    for r in range(1, shards):
        sent = mine & (need_down[:, r : r + 1] > 0.5) & (rank_down[:, r : r + 1].astype(jnp.int32) == slot)
        listed = jnp.sum(jnp.where(sent, (trace - me * per).astype(f32), 0.0), axis=0, keepdims=True)
        lists_ref[r - 1 : r, :] = listed.astype(jnp.int32)
    source = permute_of(me, lane // per, shards)
    place = jnp.where(source == 0, lane % per, rank[:1].astype(jnp.int32))
    code = jnp.where(asked[0], source * per + place, 0).astype(f32)
    found = jnp.sum(code, axis=1, keepdims=True)
    hit = jnp.sum(asked[0].astype(f32), axis=1, keepdims=True)
    found = jnp.where(hit > 0.5, found, float(every))
    down = lax.broadcasted_iota(jnp.int32, (per, LANES), 0)
    across = lax.broadcasted_iota(jnp.int32, (per, LANES), 1)
    turned = jnp.sum(jnp.where(down == across, jnp.broadcast_to(found, (per, LANES)), 0.0), axis=0, keepdims=True)
    places_ref[...] = turned.astype(jnp.int32)


def add_offset(reach, position, begin, source, values_ref, axial_ref, acc_ref):
    elements, _, block = acc_ref.shape
    values = values_ref[:, source : source + reach].reshape(elements * reach, block)
    product = dot(values, axial_ref[position * block : (position + 1) * block])
    acc_ref[:, begin : begin + reach] += product.reshape(elements, reach, block)


def near_kernel(step, vectors, unroll, *refs):
    refs = list(refs)
    here_ref, diag_ref, axial_ref = refs[:3]
    if step == 2:
        start_ref, acc_ref, ext = refs[3:]
    elif step == 3:
        acc_ref, gram_ref, copy_ref, ext, wide = refs[3:]
        gram_ref[...] = jnp.zeros_like(gram_ref)
    else:
        acc_ref, ext = refs[3:]
    elements, size, block = here_ref.shape

    def element(e):
        own = here_ref[e]
        total = dot(own, diag_ref[e])
        if step == 3:
            gram_ref[...] += across(own, own)
            write_wide(wide, of_element(wide, e, elements), own.astype(f32))
        else:
            total -= shift_center * own.astype(f32)
        if step == 2:
            total -= (half_width / 2.0) * start_ref[e].astype(f32)
        acc_ref[e] = total

    each(elements, element, unroll)
    if unroll > 1:
        for offset in [*range(-HW, 0), *range(1, HW + 1)]:
            shift = abs(offset) * vectors
            if shift < size:
                begin, source = (shift, 0) if offset < 0 else (0, shift)
                position = offset + HW - (offset > 0)
                add_offset(size - shift, position, begin, source, here_ref, axial_ref, acc_ref)
    else:
        edge = HW * vectors

        def wider(e):
            ext[e, :edge] = jnp.zeros((edge, block), bf16)
            ext[e, edge : edge + size] = here_ref[e]
            ext[e, edge + size :] = jnp.zeros((edge, block), bf16)

        each(elements, wider)

        def offset(p):
            begin = aligned((p + jnp.where(p < HW, 0, 1)) * vectors, vectors)
            weights = axial_ref[pl.ds(aligned(p * block, block), block), :]

            def along(e):
                acc_ref[e] += dot(ext[e, pl.ds(begin, size), :], weights)

            each(elements, along)

        each(2 * HW, offset)
    if step == 3:

        def narrow(index):
            copy_ref[index, :] = read_wide(wide, index).astype(bf16)

        each_tile(copy_ref.shape[0], ROW_TILE, narrow)


def middle_kernel(side, vectors, near_ref, edge_ref, axial_ref, acc_ref):
    del near_ref
    size = acc_ref.shape[1]
    edge = edge_ref.shape[1]
    for layers in range(1, HW + 1):
        reach = layers * vectors
        if side == 0:
            add_offset(reach, HW - layers, 0, edge - reach, edge_ref, axial_ref, acc_ref)
        else:
            add_offset(reach, HW + layers - 1, size - reach, 0, edge_ref, axial_ref, acc_ref)


def across(a, b):
    return lax.dot_general(a, b, (((1,), (1,)), ((), ())), preferred_element_type=f32)


def far_kernel(step, shards, elements, unroll, *refs):
    refs = list(refs)
    take = lambda n: [refs.pop(0) for _ in range(n)]
    places_ref, lists_ref, near_ref, traces_ref = take(4)
    arrived_refs = take(shards - 1)
    (face_ref,) = take(1)
    if step == 3:
        here_ref, gram_ref, out_ref, projected = take(4)
        projected[...] = jnp.zeros_like(projected)
    else:
        selector_ref, out_ref, out_low_ref, out_high_ref, out_traces_ref = take(5)
        sent_refs = take(shards - 1)
    scale = {1: 1.0 / half_width, 2: 2.0 / half_width, 3: 1.0}[step]

    def element(e):
        lifted = lifted_rows(e, places_ref, traces_ref, arrived_refs)
        total = (near_ref[e] + dot(lifted, face_ref[e])) * scale
        if step == 3:
            own = here_ref[e]
            upper = total.astype(bf16)
            lower = (total - upper.astype(f32)).astype(bf16)
            projected[...] += across(own, upper) + across(own, lower)
            return
        new = total.astype(bf16)
        keep_rows(e, new, out_ref, out_low_ref, out_high_ref)
        store_traces(e, dot(new, selector_ref[...]), out_traces_ref)

    each(elements, element, unroll)
    if step != 3:
        pick_traces(lists_ref, out_traces_ref, sent_refs, unroll)
        return

    size = projected.shape[0]
    vectors = out_ref.shape[0] // 2
    down = lax.broadcasted_iota(jnp.int32, (size, size), 0)
    over = lax.broadcasted_iota(jnp.int32, (size, size), 1)
    keep = down // vectors == over // vectors
    group = (
        lax.broadcasted_iota(jnp.int32, (size, LANES), 0) % vectors
        == lax.broadcasted_iota(jnp.int32, (size, LANES), 1)
    ).astype(f32)
    for place, ref in enumerate((gram_ref, projected)):
        value = jnp.where(keep, ref[...], 0.0).reshape(size // vectors, vectors, size).sum(0)
        value = jnp.dot(value, group, precision=lax.Precision.HIGHEST, preferred_element_type=f32)
        out_ref[place * vectors : (place + 1) * vectors] = value


def shape(dims, dtype=bf16):
    return jax.ShapeDtypeStruct(dims, dtype)


def params(rows):
    return pltpu.CompilerParams(vmem_limit_bytes=14 * 2**20 + rows * 12 * 2**10)


def rotate(value, axis, shift):
    count = lax.axis_size(axis)
    return lax.ppermute(value, axis, [(i, (i + shift) % count) for i in range(count)])


def send_traces(value, r):
    count = lax.axis_size("xs")
    if paired(count):
        return lax.ppermute(value, "xs", [(i, i ^ r) for i in range(count)])
    return rotate(value, "xs", r)


def add_over(value, axis):
    count = lax.axis_size(axis)
    if not paired(count):
        return lax.psum(value, axis)
    step = 1
    while step < count:
        far = lambda distance: lax.ppermute(value, axis, [(i, i ^ distance) for i in range(count)])
        if (count // step).bit_length() % 2 == 0:
            value = value + far(step)
            step *= 2
        else:
            value = (value + far(step)) + (far(2 * step) + far(3 * step))
            step *= 4
    return value


def local(start_vectors, diag_blocks, face_blocks, axial_blocks, neighbor_ids, neighbor_face, face_mask):
    layers, vectors, elements, block = start_vectors.shape
    shards = lax.axis_size("xs")
    me = lax.axis_index("xs").astype(jnp.int32)
    per = elements * F
    rows = layers * vectors * elements
    face_flat = face_blocks.reshape(elements, F * TR, block)
    axial_flat = axial_blocks.reshape(2 * HW * block, block)
    selector = trace_selector(block)

    codes = jnp.where(face_mask == 1, neighbor_ids * F + neighbor_face, -1).reshape(per, 1)
    codes = jnp.broadcast_to(codes, (per, LANES)).astype(jnp.int32)
    back = lambda r: send_traces(codes, r if paired(shards) else shards - r)
    all_codes = [codes] + [back(r) for r in range(1, shards)]
    lists, places, level = pl.pallas_call(
        pattern_kernel,
        out_shape=[shape((8, LANES), jnp.int32), shape((1, LANES), jnp.int32), shape((1, LANES), jnp.int32)],
        in_specs=[VMEM] * shards + [SMEM],
        out_specs=[VMEM] * 3,
        compiler_params=params(rows),
        name="pattern",
    )(*all_codes, me.reshape(1))

    start_flat = start_vectors.reshape(rows, block)
    size, edge = layers * vectors, HW * vectors
    field, side = shape((elements, size, block)), shape((elements, edge, block))
    start, low, high, traces = pl.pallas_call(
        functools.partial(opening_kernel, elements),
        out_shape=[field, side, side, shape((per, size // 2, LANES))],
        in_specs=[ANY, VMEM],
        out_specs=[VMEM] * 4,
        scratch_shapes=[
            pltpu.VMEM((rows, block), bf16),
            pltpu.VMEM((block // LANES, rows, LANES), f32),
            pltpu.SemaphoreType.DMA((4,)),
        ],
        compiler_params=params(rows),
        name="opening",
    )(start_vectors.reshape(rows, block), selector)

    def unroll_of(caps):
        return 1 if caps[-1] == per else UNROLL if caps[-1] == CAPS[0] else UNROLL // 4

    def one_round(step, caps, here, low, high, traces, sent):
        unroll = unroll_of(caps)
        arrived = [send_traces(s, r + 1) for r, s in enumerate(sent)]
        from_low = rotate(high, "pipe", 1)
        from_high = rotate(low, "pipe", -1)
        operands = [here, diag_blocks, axial_flat] + [start] * (step == 2)
        outs = [shape((elements, size, block), f32)]
        scratch = [pltpu.VMEM((elements, size + 2 * edge, block) if unroll == 1 else (16, LANES), bf16)]
        if step == 3:
            outs += [shape((size, size), f32), shape((rows, block))]
            scratch += [pltpu.VMEM((block // LANES, rows, LANES), f32)]
        near, *more = pl.pallas_call(
            functools.partial(near_kernel, step, vectors, unroll),
            out_shape=outs,
            in_specs=[VMEM] * len(operands),
            out_specs=[VMEM] * len(outs),
            scratch_shapes=scratch,
            compiler_params=params(rows),
            cost_estimate=pl.CostEstimate(flops=14 * rows * block * block, bytes_accessed=10**7, transcendentals=0),
            name=f"near_{step}",
        )(*operands)
        for which, arriving in enumerate((from_low, from_high)):
            near = pl.pallas_call(
                functools.partial(middle_kernel, which, vectors),
                out_shape=shape((elements, size, block), f32),
                in_specs=[VMEM] * 3,
                out_specs=VMEM,
                input_output_aliases={0: 0},
                compiler_params=params(rows),
                cost_estimate=pl.CostEstimate(
                    flops=5 * rows * block * block // 2, bytes_accessed=10**7, transcendentals=0
                ),
                name=f"middle_{step}",
            )(near, arriving, axial_flat)
        operands = [places, lists, near, traces, *arrived, face_flat]
        scratch = []
        if step == 3:
            operands += [here, more[0]]
            outs = [shape((2 * vectors, LANES), f32)]
            scratch = [pltpu.VMEM((size, size), f32)]
        else:
            operands += [selector]
            outs = [field, side, side, shape((per, size // 2, LANES))]
            outs += [shape((cap, size // 2, LANES)) for cap in caps]
        results = pl.pallas_call(
            functools.partial(far_kernel, step, shards, elements, unroll),
            out_shape=outs,
            in_specs=[SMEM] * 2 + [VMEM] * (len(operands) - 2),
            out_specs=[VMEM] * len(outs),
            scratch_shapes=scratch,
            compiler_params=params(rows),
            cost_estimate=pl.CostEstimate(flops=2 * rows * block * block, bytes_accessed=10**7, transcendentals=0),
            name=f"far_{step}",
        )(*operands)
        return [more[1], *results] if step == 3 else results

    def run(cap):
        caps = [min(per, cap + MORE if r == 0 else cap) for r in range(shards - 1)]
        unroll = unroll_of(caps)
        sent = pl.pallas_call(
            functools.partial(picking_kernel, unroll),
            out_shape=[shape((cap, size // 2, LANES)) for cap in caps],
            in_specs=[SMEM, VMEM],
            out_specs=[VMEM] * (shards - 1),
            compiler_params=params(rows),
            name="picking",
        )(lists, traces)
        first, *rest = one_round(1, caps, start, low, high, traces, sent)
        second, *rest = one_round(2, caps, first, rest[0], rest[1], rest[2], rest[3:])
        filtered, both = one_round(3, caps, second, rest[0], rest[1], rest[2], rest[3:])
        return filtered, both

    branches = [functools.partial(run, cap) for cap in (*CAPS, per)]
    filtered, both = lax.switch(level[0, 0], branches)
    both = add_over(add_over(both, "pipe"), "xs")
    count_all = float(layers * lax.axis_size("pipe") * elements * shards * block)
    both = both[:, :vectors] / count_all
    return filtered.reshape(start_vectors.shape), both[:vectors], both[vectors:]


def solution(mesh):
    in_specs = (
        P("pipe", None, "xs", None),
        P("xs", None, None),
        P("xs", None, None, None),
        P(),
        P("xs", None),
        P("xs", None),
        P("xs", None),
    )
    out_specs = (P("pipe", None, "xs", None), P(), P())
    return jax.shard_map(local, mesh=mesh, in_specs=in_specs, out_specs=out_specs, check_vma=False)
```

```python
import functools

import jax
import jax.numpy as jnp
from jax import lax
from jax.experimental import pallas as pl
from jax.experimental.pallas import tpu as pltpu
from jax.sharding import PartitionSpec as P

P_SIZE = 8
F = 4
HW = 4
TR = P_SIZE * P_SIZE
LANES = 128
CAPS = (9, 12)
ROW_TILE = 256
UNROLL = 8
MORE = 3

shift_center = 0.3
half_width = 1.2

VMEM = pl.BlockSpec(memory_space=pltpu.VMEM)
SMEM = pl.BlockSpec(memory_space=pltpu.SMEM)
HBM = pl.BlockSpec(memory_space=pltpu.HBM)
bf16 = jnp.bfloat16
f32 = jnp.float32


def dot(a, b):
    return jnp.dot(a, b, preferred_element_type=f32)


def trace_selector(block):
    node = lax.broadcasted_iota(jnp.int32, (block, F * TR), 0)
    column = lax.broadcasted_iota(jnp.int32, (block, F * TR), 1)
    face, entry = column // TR, column % TR
    major, minor = entry // P_SIZE, entry % P_SIZE
    fixed = jnp.where(face % 2 == 0, 0, P_SIZE - 1)
    on_i = fixed * TR + major * P_SIZE + minor
    on_j = major * TR + fixed * P_SIZE + minor
    return (node == jnp.where(face < 2, on_i, on_j)).astype(bf16)


def left_half(shape):
    return lax.broadcasted_iota(jnp.int32, shape, len(shape) - 1) < TR


def read_wide(ref, index):
    return jnp.concatenate([ref[k, index, :] for k in range(ref.shape[0])], axis=1)


def write_wide(ref, index, value):
    for k in range(ref.shape[0]):
        ref[k, index, :] = value[:, k * LANES : (k + 1) * LANES]


def of_element(ref, e, elements):
    return pl.ds(e, ref.shape[1] // elements, stride=elements)


def store_traces(e, values, traces_ref):
    half = values.shape[0] // 2
    for pair in range(F // 2):
        a = values[:half, pair * LANES : (pair + 1) * LANES]
        b = values[half:, pair * LANES : (pair + 1) * LANES]
        left = left_half(a.shape)
        traces_ref[e * F + 2 * pair] = jnp.where(left, a, pltpu.roll(b, TR, 1)).astype(bf16)
        traces_ref[e * F + 2 * pair + 1] = jnp.where(left, pltpu.roll(a, TR, 1), b).astype(bf16)


def aligned(value, multiple):
    return value if isinstance(value, int) else pl.multiple_of(value, multiple)


def each(count, body, unroll=1):
    def step(i, carry):
        body(i)
        return carry

    if unroll >= count:
        for i in range(count):
            body(i)
        return
    lax.fori_loop(0, count, step, 0, unroll=unroll)


def each_tile(rows, tile, body):
    each(rows // tile, lambda i: body(pl.ds(aligned(i * tile, tile), tile)))


def pick_traces(lists_ref, traces_ref, sent_refs, unroll):
    for r, sent in enumerate(sent_refs):

        def body(j, r=r, sent=sent):
            sent[j] = traces_ref[lists_ref[r, j]]

        each(sent.shape[0], body, sent.shape[0] if unroll > 1 else 1)


def lifted_rows(e, refs_ref, traces_ref, arrived_refs):
    per = traces_ref.shape[0]
    slots = []
    for f in range(F):
        code = refs_ref[0, e * F + f]
        source, place = code // per, code % per
        value = jnp.where(source == 0, traces_ref[place].astype(f32), 0.0)
        for shift, arrived in enumerate(arrived_refs):
            here = source == shift + 1
            value = jnp.where(here, arrived[jnp.where(here, place, 0)].astype(f32), value)
        slots.append(value)
    tops, bottoms = [], []
    for pair in range(F // 2):
        a, b = slots[2 * pair], slots[2 * pair + 1]
        left = left_half(a.shape)
        tops.append(jnp.where(left, a, pltpu.roll(b, TR, 1)))
        bottoms.append(jnp.where(left, pltpu.roll(a, TR, 1), b))
    both = jnp.concatenate([jnp.concatenate(tops, 1), jnp.concatenate(bottoms, 1)], 0)
    return both.astype(bf16)


def keep_rows(e, new, out_ref, low_ref, high_ref):
    edge = low_ref.shape[1]
    out_ref[e] = new
    low_ref[e] = new[:edge]
    high_ref[e] = new[new.shape[0] - edge :]


def opening_kernel(elements, start_hbm, selector_ref, out_ref, low_ref, high_ref, traces_ref, begun, wide, sems):
    parts = sems.shape[0]
    tile = begun.shape[0] // parts
    loads = []
    for i in range(parts):
        index = pl.ds(i * tile, tile)
        loads.append(pltpu.make_async_copy(start_hbm.at[index], begun.at[index], sems.at[i]))
        loads[-1].start()
    for i, load in enumerate(loads):
        load.wait()
        index = pl.ds(i * tile, tile)
        write_wide(wide, index, begun[index, :].astype(f32))

    def element(e):
        own = read_wide(wide, of_element(wide, e, elements)).astype(bf16)
        keep_rows(e, own, out_ref, low_ref, high_ref)
        store_traces(e, dot(own, selector_ref[...]), traces_ref)

    each(elements, element, elements)


def picking_kernel(unroll, lists_ref, traces_ref, *sent_refs):
    pick_traces(lists_ref, traces_ref, sent_refs, unroll)


def paired(shards):
    return shards & (shards - 1) == 0


def asker_of(me, r, shards):
    return me ^ r if paired(shards) else lax.rem(me + r, shards)


def permute_of(asker, owner, shards):
    return asker ^ owner if paired(shards) else lax.rem(asker + shards - owner, shards)


def pattern_kernel(*refs):
    codes_refs, (me_ref, lists_ref, places_ref, level_ref) = refs[:-4], refs[-4:]
    shards = len(codes_refs)
    per = codes_refs[0].shape[0]
    every = shards * per
    me = me_ref[0]
    lane = lax.broadcasted_iota(jnp.int32, (per, every), 1)
    asked = [codes[:, :1] == lane for codes in codes_refs]
    need = jnp.concatenate(
        [jnp.max(a.astype(f32), axis=0, keepdims=True) for a in asked]
        + [jnp.zeros((8 - shards % 8, every), f32)] * (shards % 8 != 0),
        axis=0,
    ).astype(bf16)
    row = lax.broadcasted_iota(jnp.int32, (every, every), 0)
    column = lax.broadcasted_iota(jnp.int32, (every, every), 1)
    same = row // per == column // per
    before = (same & (row < column)).astype(bf16)
    rank = dot(need, before)
    total = dot(need, same.astype(bf16))
    over = (((0,), (1,)), ((), ()))
    rank_down = lax.dot_general(before, need, over, preferred_element_type=f32)
    need_down = lax.dot_general((row == column).astype(bf16), need, over, preferred_element_type=f32)
    owner = lax.broadcasted_iota(jnp.int32, total.shape, 1) // per
    number = lax.broadcasted_iota(jnp.int32, total.shape, 0)
    permute = permute_of(asker_of(me, number, shards), owner, shards)
    weighed = jnp.where(permute == 1, total - MORE, total)
    weighed = jnp.where((permute == 0) | (number >= shards), 0.0, weighed)
    most = jnp.max(jnp.max(weighed, axis=1, keepdims=True), axis=0, keepdims=True)
    level = sum((most > cap).astype(jnp.int32) for cap in CAPS)
    level_ref[...] = jnp.broadcast_to(level, level_ref.shape)
    trace = lax.broadcasted_iota(jnp.int32, (every, LANES), 0)
    slot = lax.broadcasted_iota(jnp.int32, (every, LANES), 1)
    mine = trace // per == me
    lists_ref[...] = jnp.zeros_like(lists_ref)
    for r in range(1, shards):
        sent = mine & (need_down[:, r : r + 1] > 0.5) & (rank_down[:, r : r + 1].astype(jnp.int32) == slot)
        listed = jnp.sum(jnp.where(sent, (trace - me * per).astype(f32), 0.0), axis=0, keepdims=True)
        lists_ref[r - 1 : r, :] = listed.astype(jnp.int32)
    source = permute_of(me, lane // per, shards)
    place = jnp.where(source == 0, lane % per, rank[:1].astype(jnp.int32))
    code = jnp.where(asked[0], source * per + place, 0).astype(f32)
    found = jnp.sum(code, axis=1, keepdims=True)
    hit = jnp.sum(asked[0].astype(f32), axis=1, keepdims=True)
    found = jnp.where(hit > 0.5, found, float(every))
    down = lax.broadcasted_iota(jnp.int32, (per, LANES), 0)
    across = lax.broadcasted_iota(jnp.int32, (per, LANES), 1)
    turned = jnp.sum(jnp.where(down == across, jnp.broadcast_to(found, (per, LANES)), 0.0), axis=0, keepdims=True)
    places_ref[...] = turned.astype(jnp.int32)


def add_offset(reach, position, begin, source, values_ref, axial_ref, acc_ref):
    elements, _, block = acc_ref.shape
    values = values_ref[:, source : source + reach].reshape(elements * reach, block)
    product = dot(values, axial_ref[position * block : (position + 1) * block])
    acc_ref[:, begin : begin + reach] += product.reshape(elements, reach, block)


def add_offset_of(reach, position, begin, source, values_ref, axial_ref, acc_ref, e):
    block = acc_ref.shape[2]
    weights = axial_ref[position * block : (position + 1) * block]
    acc_ref[e, begin : begin + reach] += dot(values_ref[e, source : source + reach], weights)


def near_kernel(step, vectors, unroll, *refs):
    refs = list(refs)
    here_ref, diag_ref, axial_ref = refs[:3]
    if step == 2:
        start_ref, acc_ref, ext = refs[3:]
    elif step == 3:
        acc_ref, gram_ref, copy_ref, ext, wide = refs[3:]
        gram_ref[...] = jnp.zeros_like(gram_ref)
    else:
        acc_ref, ext = refs[3:]
    elements, size, block = here_ref.shape

    def element(e):
        own = here_ref[e]
        total = dot(own, diag_ref[e])
        if step == 3:
            gram_ref[...] += across(own, own)
            write_wide(wide, of_element(wide, e, elements), own.astype(f32))
        else:
            total -= shift_center * own.astype(f32)
        if step == 2:
            total -= (half_width / 2.0) * start_ref[e].astype(f32)
        acc_ref[e] = total

    each(elements, element, unroll)
    if unroll > 1:
        for offset in [*range(-HW, 0), *range(1, HW + 1)]:
            shift = abs(offset) * vectors
            if shift < size:
                begin, source = (shift, 0) if offset < 0 else (0, shift)
                position = offset + HW - (offset > 0)
                add_offset(size - shift, position, begin, source, here_ref, axial_ref, acc_ref)
    else:
        edge = HW * vectors

        def wider(e):
            ext[e, :edge] = jnp.zeros((edge, block), bf16)
            ext[e, edge : edge + size] = here_ref[e]
            ext[e, edge + size :] = jnp.zeros((edge, block), bf16)

        each(elements, wider)

        def offset(p):
            begin = aligned((p + jnp.where(p < HW, 0, 1)) * vectors, vectors)
            weights = axial_ref[pl.ds(aligned(p * block, block), block), :]

            def along(e):
                acc_ref[e] += dot(ext[e, pl.ds(begin, size), :], weights)

            each(elements, along)

        each(2 * HW, offset)
    if step == 3:

        def narrow(index):
            copy_ref[index, :] = read_wide(wide, index).astype(bf16)

        each_tile(copy_ref.shape[0], ROW_TILE, narrow)


def middle_kernel(side, vectors, unroll, near_ref, edge_ref, axial_ref, acc_ref):
    del near_ref
    size = acc_ref.shape[1]
    edge = edge_ref.shape[1]
    for layers in range(1, HW + 1):
        reach = layers * vectors
        if side == 0:
            terms = (reach, HW - layers, 0, edge - reach, edge_ref, axial_ref, acc_ref)
        else:
            terms = (reach, HW + layers - 1, size - reach, 0, edge_ref, axial_ref, acc_ref)
        if unroll > 1:
            add_offset(*terms)
        else:
            each(acc_ref.shape[0], functools.partial(add_offset_of, *terms))


def across(a, b):
    return lax.dot_general(a, b, (((1,), (1,)), ((), ())), preferred_element_type=f32)


def far_kernel(step, shards, elements, unroll, *refs):
    refs = list(refs)
    take = lambda n: [refs.pop(0) for _ in range(n)]
    places_ref, lists_ref, near_ref, traces_ref = take(4)
    arrived_refs = take(shards - 1)
    (face_ref,) = take(1)
    if step == 3:
        here_ref, gram_ref, out_ref, projected = take(4)
        projected[...] = jnp.zeros_like(projected)
    else:
        selector_ref, out_ref, out_low_ref, out_high_ref, out_traces_ref = take(5)
        sent_refs = take(shards - 1)
    scale = {1: 1.0 / half_width, 2: 2.0 / half_width, 3: 1.0}[step]

    def element(e):
        lifted = lifted_rows(e, places_ref, traces_ref, arrived_refs)
        total = (near_ref[e] + dot(lifted, face_ref[e])) * scale
        if step == 3:
            own = here_ref[e]
            upper = total.astype(bf16)
            lower = (total - upper.astype(f32)).astype(bf16)
            projected[...] += across(own, upper) + across(own, lower)
            return
        new = total.astype(bf16)
        keep_rows(e, new, out_ref, out_low_ref, out_high_ref)
        store_traces(e, dot(new, selector_ref[...]), out_traces_ref)

    each(elements, element, unroll)
    if step != 3:
        pick_traces(lists_ref, out_traces_ref, sent_refs, unroll)
        return

    size = projected.shape[0]
    vectors = out_ref.shape[0] // 2
    down = lax.broadcasted_iota(jnp.int32, (size, size), 0)
    over = lax.broadcasted_iota(jnp.int32, (size, size), 1)
    keep = down // vectors == over // vectors
    group = (
        lax.broadcasted_iota(jnp.int32, (size, LANES), 0) % vectors
        == lax.broadcasted_iota(jnp.int32, (size, LANES), 1)
    ).astype(f32)
    for place, ref in enumerate((gram_ref, projected)):
        value = jnp.where(keep, ref[...], 0.0).reshape(size // vectors, vectors, size).sum(0)
        value = jnp.dot(value, group, precision=lax.Precision.HIGHEST, preferred_element_type=f32)
        out_ref[place * vectors : (place + 1) * vectors] = value


def shape(dims, dtype=bf16):
    return jax.ShapeDtypeStruct(dims, dtype)


def params(rows):
    return pltpu.CompilerParams(vmem_limit_bytes=14 * 2**20 + rows * 12 * 2**10)


def rotate(value, axis, shift):
    count = lax.axis_size(axis)
    return lax.ppermute(value, axis, [(i, (i + shift) % count) for i in range(count)])


def send_traces(value, r):
    count = lax.axis_size("xs")
    if paired(count):
        return lax.ppermute(value, "xs", [(i, i ^ r) for i in range(count)])
    return rotate(value, "xs", r)


def add_over(value, axis):
    count = lax.axis_size(axis)
    if not paired(count):
        return lax.psum(value, axis)
    step = 1
    while step < count:
        far = lambda distance: lax.ppermute(value, axis, [(i, i ^ distance) for i in range(count)])
        if (count // step).bit_length() % 2 == 0:
            value = value + far(step)
            step *= 2
        else:
            value = (value + far(step)) + (far(2 * step) + far(3 * step))
            step *= 4
    return value


def local(start_vectors, diag_blocks, face_blocks, axial_blocks, neighbor_ids, neighbor_face, face_mask):
    layers, vectors, elements, block = start_vectors.shape
    shards = lax.axis_size("xs")
    me = lax.axis_index("xs").astype(jnp.int32)
    per = elements * F
    rows = layers * vectors * elements
    face_flat = face_blocks.reshape(elements, F * TR, block)
    axial_flat = axial_blocks.reshape(2 * HW * block, block)
    selector = trace_selector(block)

    codes = jnp.where(face_mask == 1, neighbor_ids * F + neighbor_face, -1).reshape(per, 1)
    codes = jnp.broadcast_to(codes, (per, LANES)).astype(jnp.int32)
    back = lambda r: send_traces(codes, r if paired(shards) else shards - r)
    all_codes = [codes] + [back(r) for r in range(1, shards)]
    lists, places, level = pl.pallas_call(
        pattern_kernel,
        out_shape=[shape((8, LANES), jnp.int32), shape((1, LANES), jnp.int32), shape((1, LANES), jnp.int32)],
        in_specs=[VMEM] * shards + [SMEM],
        out_specs=[VMEM] * 3,
        compiler_params=params(rows),
        name="pattern",
    )(*all_codes, me.reshape(1))

    start_flat = start_vectors.reshape(rows, block)
    size, edge = layers * vectors, HW * vectors
    field, side = shape((elements, size, block)), shape((elements, edge, block))
    start, low, high, traces = pl.pallas_call(
        functools.partial(opening_kernel, elements),
        out_shape=[field, side, side, shape((per, size // 2, LANES))],
        in_specs=[HBM, VMEM],
        out_specs=[VMEM] * 4,
        scratch_shapes=[
            pltpu.VMEM((rows, block), bf16),
            pltpu.VMEM((block // LANES, rows, LANES), f32),
            pltpu.SemaphoreType.DMA((4,)),
        ],
        compiler_params=params(rows),
        name="opening",
    )(start_vectors.reshape(rows, block), selector)

    def unroll_of(caps):
        return 1 if caps[-1] == per else UNROLL if caps[-1] == CAPS[0] else UNROLL // 4

    def one_round(step, caps, here, low, high, traces, sent):
        unroll = unroll_of(caps)
        arrived = [send_traces(s, r + 1) for r, s in enumerate(sent)]
        from_low = rotate(high, "pipe", 1)
        from_high = rotate(low, "pipe", -1)
        operands = [here, diag_blocks, axial_flat] + [start] * (step == 2)
        outs = [shape((elements, size, block), f32)]
        scratch = [pltpu.VMEM((elements, size + 2 * edge, block) if unroll == 1 else (16, LANES), bf16)]
        if step == 3:
            outs += [shape((size, size), f32), shape((rows, block))]
            scratch += [pltpu.VMEM((block // LANES, rows, LANES), f32)]
        near, *more = pl.pallas_call(
            functools.partial(near_kernel, step, vectors, unroll),
            out_shape=outs,
            in_specs=[VMEM] * len(operands),
            out_specs=[VMEM] * len(outs),
            scratch_shapes=scratch,
            compiler_params=params(rows),
            cost_estimate=pl.CostEstimate(flops=14 * rows * block * block, bytes_accessed=10**7, transcendentals=0),
            name=f"near_{step}",
        )(*operands)
        for which, arriving in enumerate((from_low, from_high)):
            near = pl.pallas_call(
                functools.partial(middle_kernel, which, vectors, unroll),
                out_shape=shape((elements, size, block), f32),
                in_specs=[VMEM] * 3,
                out_specs=VMEM,
                input_output_aliases={0: 0},
                compiler_params=params(rows),
                cost_estimate=pl.CostEstimate(
                    flops=5 * rows * block * block // 2, bytes_accessed=10**7, transcendentals=0
                ),
                name=f"middle_{step}",
            )(near, arriving, axial_flat)
        operands = [places, lists, near, traces, *arrived, face_flat]
        scratch = []
        if step == 3:
            operands += [here, more[0]]
            outs = [shape((2 * vectors, LANES), f32)]
            scratch = [pltpu.VMEM((size, size), f32)]
        else:
            operands += [selector]
            outs = [field, side, side, shape((per, size // 2, LANES))]
            outs += [shape((cap, size // 2, LANES)) for cap in caps]
        results = pl.pallas_call(
            functools.partial(far_kernel, step, shards, elements, unroll),
            out_shape=outs,
            in_specs=[SMEM] * 2 + [VMEM] * (len(operands) - 2),
            out_specs=[VMEM] * len(outs),
            scratch_shapes=scratch,
            compiler_params=params(rows),
            cost_estimate=pl.CostEstimate(flops=2 * rows * block * block, bytes_accessed=10**7, transcendentals=0),
            name=f"far_{step}",
        )(*operands)
        return [more[1], *results] if step == 3 else results

    def run(cap):
        caps = [min(per, cap + MORE if r == 0 else cap) for r in range(shards - 1)]
        unroll = unroll_of(caps)
        sent = pl.pallas_call(
            functools.partial(picking_kernel, unroll),
            out_shape=[shape((cap, size // 2, LANES)) for cap in caps],
            in_specs=[SMEM, VMEM],
            out_specs=[VMEM] * (shards - 1),
            compiler_params=params(rows),
            name="picking",
        )(lists, traces)
        first, *rest = one_round(1, caps, start, low, high, traces, sent)
        second, *rest = one_round(2, caps, first, rest[0], rest[1], rest[2], rest[3:])
        filtered, both = one_round(3, caps, second, rest[0], rest[1], rest[2], rest[3:])
        return filtered, both

    branches = [functools.partial(run, cap) for cap in (*CAPS, per)]
    filtered, both = lax.switch(level[0, 0], branches)
    both = add_over(add_over(both, "pipe"), "xs")
    count_all = float(layers * lax.axis_size("pipe") * elements * shards * block)
    both = both[:, :vectors] / count_all
    return filtered.reshape(start_vectors.shape), both[:vectors], both[vectors:]


def solution(mesh):
    in_specs = (
        P("pipe", None, "xs", None),
        P("xs", None, None),
        P("xs", None, None, None),
        P(),
        P("xs", None),
        P("xs", None),
        P("xs", None),
    )
    out_specs = (P("pipe", None, "xs", None), P(), P())
    return jax.shard_map(local, mesh=mesh, in_specs=in_specs, out_specs=out_specs, check_vma=False)
```

```python
import functools

import jax
import jax.numpy as jnp
from jax import lax
from jax.experimental import pallas as pl
from jax.experimental.pallas import tpu as pltpu
from jax.sharding import PartitionSpec as P

P_SIZE = 8
F = 4
HW = 4
TR = P_SIZE * P_SIZE
LANES = 128
CAPS = (9, 12)
ROW_TILE = 256
UNROLL = 8
OPENING_VMEM = 56 * 2**20
MORE = 3

shift_center = 0.3
half_width = 1.2

VMEM = pl.BlockSpec(memory_space=pltpu.VMEM)
SMEM = pl.BlockSpec(memory_space=pltpu.SMEM)
HBM = pl.BlockSpec(memory_space=pltpu.HBM)
bf16 = jnp.bfloat16
f32 = jnp.float32


def dot(a, b):
    return jnp.dot(a, b, preferred_element_type=f32)


def trace_selector(block):
    node = lax.broadcasted_iota(jnp.int32, (block, F * TR), 0)
    column = lax.broadcasted_iota(jnp.int32, (block, F * TR), 1)
    face, entry = column // TR, column % TR
    major, minor = entry // P_SIZE, entry % P_SIZE
    fixed = jnp.where(face % 2 == 0, 0, P_SIZE - 1)
    on_i = fixed * TR + major * P_SIZE + minor
    on_j = major * TR + fixed * P_SIZE + minor
    return (node == jnp.where(face < 2, on_i, on_j)).astype(bf16)


def left_half(shape):
    return lax.broadcasted_iota(jnp.int32, shape, len(shape) - 1) < TR


def read_wide(ref, index):
    return jnp.concatenate([ref[k, index, :] for k in range(ref.shape[0])], axis=1)


def write_wide(ref, index, value):
    for k in range(ref.shape[0]):
        ref[k, index, :] = value[:, k * LANES : (k + 1) * LANES]


def of_element(ref, e, elements):
    return pl.ds(e, ref.shape[1] // elements, stride=elements)


def store_traces(e, values, traces_ref):
    half = values.shape[0] // 2
    for pair in range(F // 2):
        a = values[:half, pair * LANES : (pair + 1) * LANES]
        b = values[half:, pair * LANES : (pair + 1) * LANES]
        left = left_half(a.shape)
        traces_ref[e * F + 2 * pair] = jnp.where(left, a, pltpu.roll(b, TR, 1)).astype(bf16)
        traces_ref[e * F + 2 * pair + 1] = jnp.where(left, pltpu.roll(a, TR, 1), b).astype(bf16)


def aligned(value, multiple):
    return value if isinstance(value, int) else pl.multiple_of(value, multiple)


def each(count, body, unroll=1):
    def step(i, carry):
        body(i)
        return carry

    if unroll >= count:
        for i in range(count):
            body(i)
        return
    lax.fori_loop(0, count, step, 0, unroll=unroll)


def each_tile(rows, tile, body):
    each(rows // tile, lambda i: body(pl.ds(aligned(i * tile, tile), tile)))


def pick_traces(lists_ref, traces_ref, sent_refs, unroll):
    for r, sent in enumerate(sent_refs):

        def body(j, r=r, sent=sent):
            sent[j] = traces_ref[lists_ref[r, j]]

        each(sent.shape[0], body, sent.shape[0] if unroll > 1 else 1)


def lifted_rows(e, refs_ref, traces_ref, arrived_refs):
    per = traces_ref.shape[0]
    slots = []
    for f in range(F):
        code = refs_ref[0, e * F + f]
        source, place = code // per, code % per
        value = jnp.where(source == 0, traces_ref[place].astype(f32), 0.0)
        for shift, arrived in enumerate(arrived_refs):
            here = source == shift + 1
            value = jnp.where(here, arrived[jnp.where(here, place, 0)].astype(f32), value)
        slots.append(value)
    tops, bottoms = [], []
    for pair in range(F // 2):
        a, b = slots[2 * pair], slots[2 * pair + 1]
        left = left_half(a.shape)
        tops.append(jnp.where(left, a, pltpu.roll(b, TR, 1)))
        bottoms.append(jnp.where(left, pltpu.roll(a, TR, 1), b))
    both = jnp.concatenate([jnp.concatenate(tops, 1), jnp.concatenate(bottoms, 1)], 0)
    return both.astype(bf16)


def keep_rows(e, new, out_ref, low_ref, high_ref):
    edge = low_ref.shape[1]
    out_ref[e] = new
    low_ref[e] = new[:edge]
    high_ref[e] = new[new.shape[0] - edge :]


def opening_kernel(elements, start_hbm, selector_ref, out_ref, low_ref, high_ref, traces_ref, begun, wide, sems):
    parts = sems.shape[0]
    tile = begun.shape[0] // parts
    loads = []
    for i in range(parts):
        index = pl.ds(i * tile, tile)
        loads.append(pltpu.make_async_copy(start_hbm.at[index], begun.at[index], sems.at[i]))
        loads[-1].start()
    for i, load in enumerate(loads):
        load.wait()
        index = pl.ds(i * tile, tile)
        write_wide(wide, index, begun[index, :].astype(f32))

    def element(e):
        own = read_wide(wide, of_element(wide, e, elements)).astype(bf16)
        keep_rows(e, own, out_ref, low_ref, high_ref)
        store_traces(e, dot(own, selector_ref[...]), traces_ref)

    each(elements, element, elements)


def picking_kernel(unroll, lists_ref, traces_ref, *sent_refs):
    pick_traces(lists_ref, traces_ref, sent_refs, unroll)


def paired(shards):
    return shards & (shards - 1) == 0


def asker_of(me, r, shards):
    return me ^ r if paired(shards) else lax.rem(me + r, shards)


def permute_of(asker, owner, shards):
    return asker ^ owner if paired(shards) else lax.rem(asker + shards - owner, shards)


def pattern_kernel(*refs):
    codes_refs, (me_ref, lists_ref, places_ref, level_ref) = refs[:-4], refs[-4:]
    shards = len(codes_refs)
    per = codes_refs[0].shape[0]
    every = shards * per
    me = me_ref[0]
    lane = lax.broadcasted_iota(jnp.int32, (per, every), 1)
    asked = [codes[:, :1] == lane for codes in codes_refs]
    need = jnp.concatenate(
        [jnp.max(a.astype(f32), axis=0, keepdims=True) for a in asked]
        + [jnp.zeros((8 - shards % 8, every), f32)] * (shards % 8 != 0),
        axis=0,
    ).astype(bf16)
    row = lax.broadcasted_iota(jnp.int32, (every, every), 0)
    column = lax.broadcasted_iota(jnp.int32, (every, every), 1)
    same = row // per == column // per
    before = (same & (row < column)).astype(bf16)
    rank = dot(need, before)
    total = dot(need, same.astype(bf16))
    over = (((0,), (1,)), ((), ()))
    rank_down = lax.dot_general(before, need, over, preferred_element_type=f32)
    need_down = lax.dot_general((row == column).astype(bf16), need, over, preferred_element_type=f32)
    owner = lax.broadcasted_iota(jnp.int32, total.shape, 1) // per
    number = lax.broadcasted_iota(jnp.int32, total.shape, 0)
    permute = permute_of(asker_of(me, number, shards), owner, shards)
    weighed = jnp.where(permute == 1, total - MORE, total)
    weighed = jnp.where((permute == 0) | (number >= shards), 0.0, weighed)
    most = jnp.max(jnp.max(weighed, axis=1, keepdims=True), axis=0, keepdims=True)
    level = sum((most > cap).astype(jnp.int32) for cap in CAPS)
    level_ref[...] = jnp.broadcast_to(level, level_ref.shape)
    trace = lax.broadcasted_iota(jnp.int32, (every, LANES), 0)
    slot = lax.broadcasted_iota(jnp.int32, (every, LANES), 1)
    mine = trace // per == me
    lists_ref[...] = jnp.zeros_like(lists_ref)
    for r in range(1, shards):
        sent = mine & (need_down[:, r : r + 1] > 0.5) & (rank_down[:, r : r + 1].astype(jnp.int32) == slot)
        listed = jnp.sum(jnp.where(sent, (trace - me * per).astype(f32), 0.0), axis=0, keepdims=True)
        lists_ref[r - 1 : r, :] = listed.astype(jnp.int32)
    source = permute_of(me, lane // per, shards)
    place = jnp.where(source == 0, lane % per, rank[:1].astype(jnp.int32))
    code = jnp.where(asked[0], source * per + place, 0).astype(f32)
    found = jnp.sum(code, axis=1, keepdims=True)
    hit = jnp.sum(asked[0].astype(f32), axis=1, keepdims=True)
    found = jnp.where(hit > 0.5, found, float(every))
    down = lax.broadcasted_iota(jnp.int32, (per, LANES), 0)
    across = lax.broadcasted_iota(jnp.int32, (per, LANES), 1)
    turned = jnp.sum(jnp.where(down == across, jnp.broadcast_to(found, (per, LANES)), 0.0), axis=0, keepdims=True)
    places_ref[...] = turned.astype(jnp.int32)


def add_offset(reach, position, begin, source, values_ref, axial_ref, acc_ref):
    elements, _, block = acc_ref.shape
    values = values_ref[:, source : source + reach].reshape(elements * reach, block)
    product = dot(values, axial_ref[position * block : (position + 1) * block])
    acc_ref[:, begin : begin + reach] += product.reshape(elements, reach, block)


def add_offset_of(reach, position, begin, source, values_ref, axial_ref, acc_ref, e):
    block = acc_ref.shape[2]
    weights = axial_ref[position * block : (position + 1) * block]
    acc_ref[e, begin : begin + reach] += dot(values_ref[e, source : source + reach], weights)


def near_kernel(step, vectors, unroll, *refs):
    refs = list(refs)
    here_ref, diag_ref, axial_ref = refs[:3]
    if step == 2:
        start_ref, acc_ref, ext = refs[3:]
    elif step == 3:
        acc_ref, gram_ref, copy_ref, ext, wide, gram = refs[3:]
        gram[...] = jnp.zeros_like(gram)
    else:
        acc_ref, ext = refs[3:]
    elements, size, block = here_ref.shape

    def element(e):
        own = here_ref[e]
        total = dot(own, diag_ref[e])
        if step == 3:
            gram[...] += across(own, own)
            write_wide(wide, of_element(wide, e, elements), own.astype(f32))
        else:
            total -= shift_center * own.astype(f32)
        if step == 2:
            total -= (half_width / 2.0) * start_ref[e].astype(f32)
        acc_ref[e] = total

    each(elements, element, unroll)
    if unroll > 1:
        for offset in [*range(-HW, 0), *range(1, HW + 1)]:
            shift = abs(offset) * vectors
            if shift < size:
                begin, source = (shift, 0) if offset < 0 else (0, shift)
                position = offset + HW - (offset > 0)
                add_offset(size - shift, position, begin, source, here_ref, axial_ref, acc_ref)
    else:
        edge = HW * vectors

        def wider(e):
            ext[e, :edge] = jnp.zeros((edge, block), bf16)
            ext[e, edge : edge + size] = here_ref[e]
            ext[e, edge + size :] = jnp.zeros((edge, block), bf16)

        each(elements, wider)

        def offset(p):
            begin = aligned((p + jnp.where(p < HW, 0, 1)) * vectors, vectors)
            weights = axial_ref[pl.ds(aligned(p * block, block), block), :]

            def along(e):
                acc_ref[e] += dot(ext[e, pl.ds(begin, size), :], weights)

            each(elements, along)

        each(2 * HW, offset)
    if step == 3:
        gram_ref[...] = layer_sum(gram[...], vectors)

        def narrow(index):
            copy_ref[index, :] = read_wide(wide, index).astype(bf16)

        each_tile(copy_ref.shape[0], ROW_TILE, narrow)


def middle_kernel(side, vectors, unroll, near_ref, edge_ref, axial_ref, acc_ref):
    del near_ref
    size = acc_ref.shape[1]
    edge = edge_ref.shape[1]
    for layers in range(1, HW + 1):
        reach = layers * vectors
        if side == 0:
            terms = (reach, HW - layers, 0, edge - reach, edge_ref, axial_ref, acc_ref)
        else:
            terms = (reach, HW + layers - 1, size - reach, 0, edge_ref, axial_ref, acc_ref)
        if unroll > 1:
            add_offset(*terms)
        else:
            each(acc_ref.shape[0], functools.partial(add_offset_of, *terms))


def across(a, b):
    return lax.dot_general(a, b, (((1,), (1,)), ((), ())), preferred_element_type=f32)


def layer_sum(value, vectors):
    size = value.shape[0]
    down = lax.broadcasted_iota(jnp.int32, (size, size), 0)
    over = lax.broadcasted_iota(jnp.int32, (size, size), 1)
    group = (
        lax.broadcasted_iota(jnp.int32, (size, LANES), 0) % vectors
        == lax.broadcasted_iota(jnp.int32, (size, LANES), 1)
    ).astype(f32)
    value = jnp.where(down // vectors == over // vectors, value, 0.0)
    value = value.reshape(size // vectors, vectors, size).sum(0)
    return jnp.dot(value, group, precision=lax.Precision.HIGHEST, preferred_element_type=f32)


def far_kernel(step, shards, elements, unroll, *refs):
    refs = list(refs)
    take = lambda n: [refs.pop(0) for _ in range(n)]
    places_ref, lists_ref, near_ref, traces_ref = take(4)
    arrived_refs = take(shards - 1)
    (face_ref,) = take(1)
    if step == 3:
        here_ref, gram_ref, out_ref, projected = take(4)
        projected[...] = jnp.zeros_like(projected)
    else:
        selector_ref, out_ref, out_low_ref, out_high_ref, out_traces_ref = take(5)
        sent_refs = take(shards - 1)
    scale = {1: 1.0 / half_width, 2: 2.0 / half_width, 3: 1.0}[step]

    def element(e):
        lifted = lifted_rows(e, places_ref, traces_ref, arrived_refs)
        total = (near_ref[e] + dot(lifted, face_ref[e])) * scale
        if step == 3:
            own = here_ref[e]
            upper = total.astype(bf16)
            lower = (total - upper.astype(f32)).astype(bf16)
            projected[...] += across(own, upper) + across(own, lower)
            return
        new = total.astype(bf16)
        keep_rows(e, new, out_ref, out_low_ref, out_high_ref)
        store_traces(e, dot(new, selector_ref[...]), out_traces_ref)

    each(elements, element, unroll)
    if step != 3:
        pick_traces(lists_ref, out_traces_ref, sent_refs, unroll)
        return

    vectors = gram_ref.shape[0]
    out_ref[:vectors] = gram_ref[...]
    out_ref[vectors:] = layer_sum(projected[...], vectors)


def shape(dims, dtype=bf16):
    return jax.ShapeDtypeStruct(dims, dtype)


def params(rows):
    return pltpu.CompilerParams(vmem_limit_bytes=14 * 2**20 + rows * 12 * 2**10)


def rotate(value, axis, shift):
    count = lax.axis_size(axis)
    return lax.ppermute(value, axis, [(i, (i + shift) % count) for i in range(count)])


def send_traces(value, r):
    count = lax.axis_size("xs")
    if paired(count):
        return lax.ppermute(value, "xs", [(i, i ^ r) for i in range(count)])
    return rotate(value, "xs", r)


def add_over(value, axis):
    count = lax.axis_size(axis)
    if not paired(count):
        return lax.psum(value, axis)
    step = 1
    while step < count:
        far = lambda distance: lax.ppermute(value, axis, [(i, i ^ distance) for i in range(count)])
        if (count // step).bit_length() % 2 == 0:
            value = value + far(step)
            step *= 2
        else:
            value = (value + far(step)) + (far(2 * step) + far(3 * step))
            step *= 4
    return value


def local(start_vectors, diag_blocks, face_blocks, axial_blocks, neighbor_ids, neighbor_face, face_mask):
    layers, vectors, elements, block = start_vectors.shape
    shards = lax.axis_size("xs")
    me = lax.axis_index("xs").astype(jnp.int32)
    per = elements * F
    rows = layers * vectors * elements
    face_flat = face_blocks.reshape(elements, F * TR, block)
    axial_flat = axial_blocks.reshape(2 * HW * block, block)
    selector = trace_selector(block)

    codes = jnp.where(face_mask == 1, neighbor_ids * F + neighbor_face, -1).reshape(per, 1)
    codes = jnp.broadcast_to(codes, (per, LANES)).astype(jnp.int32)
    back = lambda r: send_traces(codes, r if paired(shards) else shards - r)
    all_codes = [codes] + [back(r) for r in range(1, shards)]
    lists, places, level = pl.pallas_call(
        pattern_kernel,
        out_shape=[shape((8, LANES), jnp.int32), shape((1, LANES), jnp.int32), shape((1, LANES), jnp.int32)],
        in_specs=[VMEM] * shards + [SMEM],
        out_specs=[VMEM] * 3,
        compiler_params=params(rows),
        name="pattern",
    )(*all_codes, me.reshape(1))

    start_flat = start_vectors.reshape(rows, block)
    size, edge = layers * vectors, HW * vectors
    field, side = shape((elements, size, block)), shape((elements, edge, block))
    start, low, high, traces = pl.pallas_call(
        functools.partial(opening_kernel, elements),
        out_shape=[field, side, side, shape((per, size // 2, LANES))],
        in_specs=[HBM, VMEM],
        out_specs=[VMEM] * 4,
        scratch_shapes=[
            pltpu.VMEM((rows, block), bf16),
            pltpu.VMEM((block // LANES, rows, LANES), f32),
            pltpu.SemaphoreType.DMA((4,)),
        ],
        compiler_params=pltpu.CompilerParams(vmem_limit_bytes=OPENING_VMEM),
        name="opening",
    )(start_vectors.reshape(rows, block), selector)

    def unroll_of(caps):
        return 1 if caps[-1] == per else UNROLL if caps[-1] == CAPS[0] else UNROLL // 4

    def one_round(step, caps, here, low, high, traces, sent):
        unroll = unroll_of(caps)
        arrived = [send_traces(s, r + 1) for r, s in enumerate(sent)]
        from_low = rotate(high, "pipe", 1)
        from_high = rotate(low, "pipe", -1)
        operands = [here, diag_blocks, axial_flat] + [start] * (step == 2)
        outs = [shape((elements, size, block), f32)]
        scratch = [pltpu.VMEM((elements, size + 2 * edge, block) if unroll == 1 else (16, LANES), bf16)]
        if step == 3:
            outs += [shape((vectors, LANES), f32), shape((rows, block))]
            scratch += [pltpu.VMEM((block // LANES, rows, LANES), f32), pltpu.VMEM((size, size), f32)]
        near, *more = pl.pallas_call(
            functools.partial(near_kernel, step, vectors, unroll),
            out_shape=outs,
            in_specs=[VMEM] * len(operands),
            out_specs=[VMEM] * len(outs),
            scratch_shapes=scratch,
            compiler_params=params(rows),
            cost_estimate=pl.CostEstimate(flops=14 * rows * block * block, bytes_accessed=10**7, transcendentals=0),
            name=f"near_{step}",
        )(*operands)
        for which, arriving in enumerate((from_low, from_high)):
            near = pl.pallas_call(
                functools.partial(middle_kernel, which, vectors, unroll),
                out_shape=shape((elements, size, block), f32),
                in_specs=[VMEM] * 3,
                out_specs=VMEM,
                input_output_aliases={0: 0},
                compiler_params=params(rows),
                cost_estimate=pl.CostEstimate(
                    flops=5 * rows * block * block // 2, bytes_accessed=10**7, transcendentals=0
                ),
                name=f"middle_{step}",
            )(near, arriving, axial_flat)
        operands = [places, lists, near, traces, *arrived, face_flat]
        scratch = []
        if step == 3:
            operands += [here, more[0]]
            outs = [shape((2 * vectors, LANES), f32)]
            scratch = [pltpu.VMEM((size, size), f32)]
        else:
            operands += [selector]
            outs = [field, side, side, shape((per, size // 2, LANES))]
            outs += [shape((cap, size // 2, LANES)) for cap in caps]
        results = pl.pallas_call(
            functools.partial(far_kernel, step, shards, elements, unroll),
            out_shape=outs,
            in_specs=[SMEM] * 2 + [VMEM] * (len(operands) - 2),
            out_specs=[VMEM] * len(outs),
            scratch_shapes=scratch,
            compiler_params=params(rows),
            cost_estimate=pl.CostEstimate(flops=2 * rows * block * block, bytes_accessed=10**7, transcendentals=0),
            name=f"far_{step}",
        )(*operands)
        return [more[1], *results] if step == 3 else results

    def run(cap):
        caps = [min(per, cap + MORE if r == 0 else cap) for r in range(shards - 1)]
        unroll = unroll_of(caps)
        sent = pl.pallas_call(
            functools.partial(picking_kernel, unroll),
            out_shape=[shape((cap, size // 2, LANES)) for cap in caps],
            in_specs=[SMEM, VMEM],
            out_specs=[VMEM] * (shards - 1),
            compiler_params=params(rows),
            name="picking",
        )(lists, traces)
        first, *rest = one_round(1, caps, start, low, high, traces, sent)
        second, *rest = one_round(2, caps, first, rest[0], rest[1], rest[2], rest[3:])
        filtered, both = one_round(3, caps, second, rest[0], rest[1], rest[2], rest[3:])
        return filtered, both

    branches = [functools.partial(run, cap) for cap in (*CAPS, per)]
    filtered, both = lax.switch(level[0, 0], branches)
    both = add_over(add_over(both, "pipe"), "xs")
    count_all = float(layers * lax.axis_size("pipe") * elements * shards * block)
    both = both[:, :vectors] / count_all
    return filtered.reshape(start_vectors.shape), both[:vectors], both[vectors:]


def solution(mesh):
    in_specs = (
        P("pipe", None, "xs", None),
        P("xs", None, None),
        P("xs", None, None, None),
        P(),
        P("xs", None),
        P("xs", None),
        P("xs", None),
    )
    out_specs = (P("pipe", None, "xs", None), P(), P())
    return jax.shard_map(local, mesh=mesh, in_specs=in_specs, out_specs=out_specs, check_vma=False)
```
